32 devices in a mesh: parts: 2 (over x), space: 16 (over z, y, core).
Axes of the slice: x: 2, y: 2, z: 4, core: 2. Of those that a mesh axis runs over, the one named last changes fastest.
Arguments:
- forward_field: float32 [2, 16, 128, 2048], P(None, 'parts', 'space'), parts along dimension 1, may hold values from -6 to 6
- adjoint_start: float32 [2, 16, 128, 2048], P(None, 'parts', 'space'), parts along dimension 1, may hold values from -45 to 45
- permittivity: float32 [256, 2048], P(('parts', 'space')), parts along dimension 0, may hold values from 1 to 6
- wavenumbers: float32 [16], P('parts'), parts along dimension 0, may hold values from 0.25 to 0.55
- monitor_cells: int32 [128], P('parts'), parts along dimension 0, may hold values from 0 to 262143
- pml_widths: int32 [8], P('parts'), parts along dimension 0, may hold values from 6 to 19
- owner_map: int32 [32, 16], P(('parts', 'space')), parts along dimension 0, may hold values from 0 to 15, each once within a row
Outputs:
- adjoint: float32 [2, 16, 128, 2048], P(None, 'parts', 'space'), parts along dimension 1
- design_grad: float32 [32, 16, 1024], P(('parts', 'space')), parts along dimension 0
The draws below stay inside these ranges and needn't reach their ends.
There are 2 independent parts, one for each index of `parts`. The reference program is written for one: setup_inputs(seed, part) draws one part's arguments, and reference() takes and returns one part's arrays. A program takes and returns all parts, laid end to end along the dimension named above; each array names one. Nothing has to cross between parts.
Inputs may be any that keep to these rules, and one draw needn't show every extreme that they name: Each row of owner_map names every index 0 to 15 once.
All inputs are finite; a program needn't handle non-finite values.
Results may differ from the reference program's by a relative error of at most 0.00015.
Values sent between devices are 32-bit elements; how exact they have to be, the bound alone decides.
A program may use at most 64 MiB of HBM per device.

```python
import math
import jax
import jax.numpy as jnp
from jax import lax

W = 8
CX = 8
NY = 2048
M = 64
ITERS = 2
TILES = 16
NX = 128
BY = 128


def draw_adjoint_start(key, part):
    key = jax.random.fold_in(key, 7)
    key_vals, key_rows, key_cols = jax.random.split(key, 3)
    position = jnp.arange(NX).astype(jnp.float32) / max(NX - 1, 1) - 0.5
    growth = jnp.exp(jnp.log(3.0) * position)
    values = jnp.clip(jax.random.normal(key_vals, (2, W, NX, NY), jnp.float32), -5.0, 5.0)
    row_scale = jnp.exp(jax.random.uniform(key_rows, (NX,), jnp.float32, jnp.log(0.5), jnp.log(1.65)))
    col_scale = jnp.exp(jax.random.uniform(key_cols, (NY,), jnp.float32, jnp.log(0.3), jnp.log(3.0)))
    return values * (growth * row_scale)[:, None] * col_scale[None, :]


def plant(result, rng, smallest, top_value):
    shape = result.shape
    index_at = [jax.random.randint(jax.random.fold_in(rng, axis), (), 0, shape[axis]) for axis in range(len(shape))]
    result = result.at[tuple(index_at)].set(smallest)
    longest = shape.index(max(shape))
    index_at[longest] = (index_at[longest] + 1) % shape[longest]
    return result.at[tuple(index_at)].set(top_value)


def level_of(key, extent, cuts, smallest, largest):
    factor_of, own = 1.0, jax.random.fold_in(key, 6)
    for dim, shards_of in cuts:
        steps = jnp.exp(jax.random.uniform(jax.random.fold_in(own, dim), (shards_of,), jnp.float32, smallest / len(cuts), largest / len(cuts)))
        factor_of = factor_of * jnp.repeat(steps, extent[dim] // shards_of).reshape([-1 if axis == dim else 1 for axis in range(len(extent))])
    return factor_of


def scatter_about(own_key, dims, spread, reach, cuts=(), kind=jnp.bfloat16):
    entries = jax.random.normal(own_key, dims, jnp.float32) * spread
    if len(cuts) > 0:
        entries = level_of(own_key, dims, cuts, -0.22, 0.18) * entries
    return jnp.clip(entries, min=-reach, max=reach).astype(kind)


def setup_inputs(seed: int = 0, part: int = 0) -> dict:
    key_of = jax.random.split(jax.random.key(seed), 8)
    own_keys = jax.random.split(jax.random.fold_in(key_of[7], part), 8)
    forward_field = scatter_about(own_keys[0], (2, W, NX, NY), 1.0, 6.0, ((2, 16),), jnp.float32)
    adjoint_start = draw_adjoint_start(jax.random.fold_in(jax.random.fold_in(key_of[7], part), 71), part)
    permittivity = jnp.clip(1.0 + 5.0 * jax.random.uniform(own_keys[2], (NX, NY), jnp.float32) ** level_of(own_keys[2], (NX, NY), ((0, 16),), -0.2, 0.2), 1.0, 6.0)
    wavenumbers = jnp.clip(jnp.exp(jax.random.uniform(own_keys[3], (W,), jnp.float32, math.log(0.25), math.log(0.55))), 0.25, 0.55)
    monitor_cells = plant(jax.random.randint(own_keys[4], (M,), 0, NX * NY), jax.random.fold_in(own_keys[4], 1), 0, (NX * NY) - 1).astype(jnp.int32)
    pml_widths = plant(jax.random.randint(own_keys[5], (4,), 6, 20), jax.random.fold_in(own_keys[5], 1), 6, 19).astype(jnp.int32)
    owner_map = jax.vmap(lambda own: jax.random.permutation(own, TILES))(jax.random.split(own_keys[6], TILES)).reshape((TILES, TILES)).astype(jnp.int32)
    return {"forward_field": forward_field, "adjoint_start": adjoint_start, "permittivity": permittivity, "wavenumbers": wavenumbers, "monitor_cells": monitor_cells, "pml_widths": pml_widths, "owner_map": owner_map}


SIGMA_PEAK = 4.0
MONITOR_GAIN = 4.0

def stretch(coord, low_width, high_width, total):
    lower_part = jnp.maximum(low_width - coord, 0.0) / low_width
    upper_part = jnp.maximum(coord - (total - 1.0 - high_width), 0.0) / high_width
    damping = SIGMA_PEAK * (lower_part ** 3 + upper_part ** 3)
    denominator = 1.0 + damping * damping
    return (1.0 / denominator, -damping / denominator)

def operate(padded, eps_rows, wave_sq, first_row, total_rows, widths):
    row_count = padded.shape[2]
    col_count = padded.shape[3]
    row_ids = (first_row + jnp.arange(row_count)).astype(jnp.float32)
    cen_re, cen_im = stretch(row_ids, widths[0], widths[1], total_rows)
    face_re, face_im = stretch(row_ids[:-1] + 0.5, widths[0], widths[1], total_rows)
    q_re = cen_re[:, None] * padded[0] - cen_im[:, None] * padded[1]
    q_im = cen_re[:, None] * padded[1] + cen_im[:, None] * padded[0]
    d_re = q_re[:, 1:] - q_re[:, :-1]
    d_im = q_im[:, 1:] - q_im[:, :-1]
    f_re = face_re[:, None] * d_re - face_im[:, None] * d_im
    f_im = face_re[:, None] * d_im + face_im[:, None] * d_re
    along_re = f_re[:, 1:] - f_re[:, :-1]
    along_im = f_im[:, 1:] - f_im[:, :-1]
    middle = padded[:, :, 1:-1]
    col_ids = jnp.arange(col_count).astype(jnp.float32)
    cy_re, cy_im = stretch(col_ids, widths[2], widths[3], col_count)
    hy_re, hy_im = stretch(jnp.arange(col_count + 1).astype(jnp.float32) - 0.5, widths[2], widths[3], col_count)
    p_re = cy_re * middle[0] - cy_im * middle[1]
    p_im = cy_re * middle[1] + cy_im * middle[0]
    zero_col = jnp.zeros(p_re.shape[:-1] + (1,), jnp.float32)
    p_re = jnp.concatenate([zero_col, p_re, zero_col], axis=-1)
    p_im = jnp.concatenate([zero_col, p_im, zero_col], axis=-1)
    e_re = p_re[..., 1:] - p_re[..., :-1]
    e_im = p_im[..., 1:] - p_im[..., :-1]
    g_re = hy_re * e_re - hy_im * e_im
    g_im = hy_re * e_im + hy_im * e_re
    cross_re = g_re[..., 1:] - g_re[..., :-1]
    cross_im = g_im[..., 1:] - g_im[..., :-1]
    mass_term = wave_sq[:, None, None] * eps_rows[None]
    out_re = -(along_re + cross_re) - mass_term * middle[0]
    out_im = -(along_im + cross_im) - mass_term * middle[1]
    centre = row_ids[1:-1]
    inside = ((centre >= 0.0) & (centre <= total_rows - 1.0)).astype(jnp.float32)[:, None]
    return jnp.stack([out_re * inside, out_im * inside])

def monitor_counts(monitor_cells, first_row, row_count, col_count):
    cell_rows = monitor_cells // col_count
    cell_cols = monitor_cells % col_count
    rows_hot = (cell_rows[None, :] == (first_row + jnp.arange(row_count))[:, None]).astype(jnp.float32)
    cols_hot = (cell_cols[:, None] == jnp.arange(col_count)[None, :]).astype(jnp.float32)
    return jnp.dot(rows_hot, cols_hot, preferred_element_type=jnp.float32, precision=lax.Precision.HIGHEST)

def times_field(coef, field):
    c_re = coef[0][:, None, None]
    c_im = coef[1][:, None, None]
    return jnp.stack([c_re * field[0] - c_im * field[1], c_re * field[1] + c_im * field[0]])

def inner_product(left, right):
    return jnp.stack([lax.optimization_barrier(jnp.sum(left[0] * right[0] + left[1] * right[1], axis=(1, 2))), lax.optimization_barrier(jnp.sum(left[0] * right[1] - left[1] * right[0], axis=(1, 2)))])

def energy(field):
    return lax.optimization_barrier(jnp.sum(field[0] * field[0] + field[1] * field[1], axis=(1, 2)))

def divide(top, bottom):
    denominator = bottom[0] * bottom[0] + bottom[1] * bottom[1]
    return jnp.stack([(top[0] * bottom[0] + top[1] * bottom[1]) / denominator, (top[1] * bottom[0] - top[0] * bottom[1]) / denominator])

def advance(norm_sq, tau_now, theta_now, eta_now, step_coef, direction, guide, solution):
    coef = theta_now * theta_now * divide(eta_now, step_coef)
    direction = guide + times_field(coef, direction)
    theta_new = jnp.sqrt(norm_sq) / tau_now
    shrink = 1.0 / (1.0 + theta_new * theta_new)
    tau_now = tau_now * theta_new * jnp.sqrt(shrink)
    eta_now = shrink * step_coef
    solution = solution + times_field(eta_now, direction)
    return (direction, tau_now, theta_new, eta_now, solution)

def reference(forward_field, adjoint_start, permittivity, wavenumbers, monitor_cells, pml_widths, owner_map):
    widths = pml_widths.astype(jnp.float32)
    wave_sq = wavenumbers * wavenumbers
    counts = monitor_counts(monitor_cells, 0, NX, NY)
    source = MONITOR_GAIN * counts * jnp.stack([-forward_field[0], forward_field[1]])

    def apply_op(field):
        padded = jnp.pad(field, ((0, 0), (0, 0), (1, 1), (0, 0)))
        return operate(padded, permittivity, wave_sq, -1, NX, widths)
    solution = adjoint_start
    residual = source - apply_op(solution)
    quasi = residual
    first_dir = residual
    shadow = residual
    image_now = apply_op(first_dir)
    search = image_now
    direction = jnp.zeros_like(residual)
    start_sq = energy(residual)
    tau_now = jnp.sqrt(start_sq)
    theta_now = jnp.zeros_like(start_sq)
    eta_now = jnp.zeros((2,) + start_sq.shape, jnp.float32)
    rho_now = jnp.stack([start_sq, jnp.zeros_like(start_sq)])
    for iteration in range(ITERS):
        step_coef = divide(rho_now, inner_product(shadow, search))
        quasi = quasi - times_field(step_coef, image_now)
        direction, tau_now, theta_now, eta_now, solution = advance(energy(quasi), tau_now, theta_now, eta_now, step_coef, direction, first_dir, solution)
        second_dir = first_dir - times_field(step_coef, search)
        image_now = apply_op(second_dir)
        quasi = quasi - times_field(step_coef, image_now)
        direction, tau_now, theta_now, eta_now, solution = advance(energy(quasi), tau_now, theta_now, eta_now, step_coef, direction, second_dir, solution)
        if iteration + 1 < ITERS:
            rho_new = inner_product(shadow, quasi)
            ratio_coef = divide(rho_new, rho_now)
            rho_now = rho_new
            first_dir = quasi + times_field(ratio_coef, second_dir)
            second_image = image_now
            image_now = apply_op(first_dir)
            search = image_now + times_field(ratio_coef, second_image + times_field(ratio_coef, search))
    gradient = -2.0 * lax.optimization_barrier(jnp.sum(wave_sq[:, None, None] * (solution[0] * forward_field[0] - solution[1] * forward_field[1]), axis=0))
    blocks = gradient.reshape(TILES, CX, TILES, BY).transpose(0, 2, 1, 3).reshape(TILES, TILES, CX * BY)
    tile_ids = jnp.arange(TILES)
    inverse = lax.optimization_barrier(jnp.sum((owner_map[:, None, :] == tile_ids[None, :, None]).astype(jnp.int32) * tile_ids[None, None, :], axis=2))
    owned = jnp.take_along_axis(blocks, inverse[:, :, None].astype(jnp.int32), axis=1)
    return (solution, owned.transpose(1, 0, 2))
```

```python
import functools

import jax
import jax.numpy as jnp
from jax import lax
from jax.experimental import pallas as pl
from jax.experimental.pallas import tpu as pltpu
from jax.sharding import PartitionSpec as P

ITERS = 2
SIGMA_PEAK = 4.0
MONITOR_GAIN = 4.0
SHIFT = 4.0
LANES = 128
DEPTH = 4
BASIS = 5
MESH = pl.DeviceIdType.MESH


def stretch(coord, low_width, high_width, total):
    lower_part = jnp.maximum(low_width - coord, 0.0) / low_width
    upper_part = jnp.maximum(coord - (total - 1.0 - high_width), 0.0) / high_width
    damping = SIGMA_PEAK * (
        lower_part * lower_part * lower_part + upper_part * upper_part * upper_part
    )
    denominator = 1.0 + damping * damping
    return (1.0 / denominator, -damping / denominator)


def cmul(a, b):
    return (a[0] * b[0] - a[1] * b[1], a[0] * b[1] + a[1] * b[0])


def cadd(a, b):
    return (a[0] + b[0], a[1] + b[1])


def csub(a, b):
    return (a[0] - b[0], a[1] - b[1])


def cdiv(top, bottom):
    d = bottom[0] * bottom[0] + bottom[1] * bottom[1]
    return (
        (top[0] * bottom[0] + top[1] * bottom[1]) / d,
        (top[1] * bottom[0] - top[0] * bottom[1]) / d,
    )


def three_point(coord, low, high, total):
    below = stretch(coord - 1.0, low, high, total)
    here = stretch(coord, low, high, total)
    above = stretch(coord + 1.0, low, high, total)
    face_low = stretch(coord - 0.5, low, high, total)
    face_high = stretch(coord + 0.5, low, high, total)
    return (
        cmul(face_low, below),
        cmul(cadd(face_low, face_high), here),
        cmul(face_high, above),
    )


def poly_dot(left, right, gram):
    total = None
    for i, a in enumerate(left):
        for j, b in enumerate(right):
            if i <= j:
                g = gram[(i, j)]
            else:
                g = (gram[(j, i)][0], -gram[(j, i)][1])
            term = cmul(cmul((a[0], -a[1]), b), g)
            total = term if total is None else cadd(total, term)
    return total


def poly_energy(q, gram):
    total = None
    for i, a in enumerate(q):
        term = (a[0] * a[0] + a[1] * a[1]) * gram[(i, i)][0]
        total = term if total is None else total + term
        for j in range(i + 1, len(q)):
            b = q[j]
            c_re = a[0] * b[0] + a[1] * b[1]
            c_im = a[0] * b[1] - a[1] * b[0]
            g = gram[(i, j)]
            total = total + 2.0 * (c_re * g[0] - c_im * g[1])
    return total


def poly_scale(c, p):
    return [cmul(c, a) for a in p]


def poly_add(p, q):
    out = []
    for i in range(max(len(p), len(q))):
        if i >= len(p):
            out.append(q[i])
        elif i >= len(q):
            out.append(p[i])
        else:
            out.append(cadd(p[i], q[i]))
    return out


def poly_sub(p, q):
    return poly_add(p, [(-a[0], -a[1]) for a in q])


def poly_image(p):
    raised = [None] + list(p)
    out = []
    for i in range(len(p) + 1):
        if i == 0:
            out.append((SHIFT * p[0][0], SHIFT * p[0][1]))
        elif i == len(p):
            out.append(raised[i])
        else:
            out.append((raised[i][0] + SHIFT * p[i][0], raised[i][1] + SHIFT * p[i][1]))
    return out


def krylov_weights(gram, one, zero):
    unit = (one, zero)
    residual = [unit]
    image = poly_image(residual)
    update = None
    quasi, first_dir, search = residual, residual, image
    direction = None
    start_sq = gram[(0, 0)][0]
    tau = jnp.sqrt(start_sq)
    theta, eta = zero, (zero, zero)
    rho = (start_sq, zero)

    def advance(norm_sq, tau, theta, eta, step, direction, guide, update):
        if direction is None:
            direction = guide
        else:
            ratio = cdiv(eta, step)
            coef = (theta * theta * ratio[0], theta * theta * ratio[1])
            direction = poly_add(guide, poly_scale(coef, direction))
        theta = jnp.sqrt(norm_sq) / tau
        shrink = 1.0 / (1.0 + theta * theta)
        tau = tau * theta * jnp.sqrt(shrink)
        eta = (shrink * step[0], shrink * step[1])
        move = poly_scale(eta, direction)
        update = move if update is None else poly_add(update, move)
        return direction, tau, theta, eta, update

    for iteration in range(ITERS):
        step = cdiv(rho, poly_dot(residual, search, gram))
        quasi = poly_sub(quasi, poly_scale(step, image))
        norm_sq = jnp.maximum(poly_energy(quasi, gram), 0.0)
        direction, tau, theta, eta, update = advance(
            norm_sq, tau, theta, eta, step, direction, first_dir, update
        )
        second_dir = poly_sub(first_dir, poly_scale(step, search))
        second_image = poly_image(second_dir)
        quasi = poly_sub(quasi, poly_scale(step, second_image))
        norm_sq = jnp.maximum(poly_energy(quasi, gram), 0.0)
        direction, tau, theta, eta, update = advance(
            norm_sq, tau, theta, eta, step, direction, second_dir, update
        )
        if iteration + 1 < ITERS:
            rho_new = poly_dot(residual, quasi, gram)
            beta = cdiv(rho_new, rho)
            rho = rho_new
            first_dir = poly_add(quasi, poly_scale(beta, second_dir))
            image = poly_image(first_dir)
            search = poly_add(
                image, poly_scale(beta, poly_add(second_image, poly_scale(beta, search)))
            )
    return update


def kernel(
    n, f_in, s_in, eps_in, wave_in, cell_in, pml_in, owner_in, adj_out, grad_out,
    S, F, V, E, CN, RC, CC, part_out, part_in, tiles, ordered, tiles_in,
    edge_send, edge_recv, sum_send, sum_recv, tile_send, tile_recv,
):
    waves, rows, cols = s_in.shape[1], s_in.shape[2], s_in.shape[3]
    blocks = cols // LANES
    width = cols // n
    me = lax.axis_index("space")
    part = lax.axis_index("parts")
    first = me * rows
    total = rows * n
    up, down = me - 1, me + 1
    has_up, has_down = me > 0, me < n - 1

    barrier = pltpu.get_barrier_semaphore()

    @pl.loop(1, n)
    def _(d):
        pl.semaphore_signal(
            barrier, inc=1, device_id=(part, lax.rem(me + d, n)), device_id_type=MESH
        )

    def at(b):
        return pl.ds(pl.multiple_of(b * LANES, LANES), LANES)

    @pl.loop(0, blocks)
    def _(b):
        for c in range(2):
            S[c, pl.ds(1, rows), :, at(b)] = jnp.swapaxes(s_in[c, :, :, at(b)], 0, 1)

    for r in range(rows):
        E[DEPTH + r] = eps_in[pl.ds(r, 1), :]

    def edge(slot, src, dst, target):
        return pltpu.make_async_remote_copy(
            src_ref=src, dst_ref=dst, send_sem=edge_send.at[slot], recv_sem=edge_recv.at[slot],
            device_id=(part, target), device_id_type=MESH,
        )

    V0 = V.at[0]
    lo, hi = DEPTH, DEPTH + rows
    to_up = [
        edge(0, S.at[:, 1], S.at[:, rows + 1], up),
        edge(1, E.at[pl.ds(lo, DEPTH)], E.at[pl.ds(hi, DEPTH)], up),
        edge(2, V0.at[:, pl.ds(lo + 1, DEPTH - 1)], V0.at[:, pl.ds(hi + 1, DEPTH - 1)], up),
        edge(3, V0.at[:, lo], V0.at[:, hi], up),
    ]
    to_down = [
        edge(4, S.at[:, rows], S.at[:, 0], down),
        edge(5, E.at[pl.ds(hi - DEPTH, DEPTH)], E.at[pl.ds(0, DEPTH)], down),
        edge(6, V0.at[:, pl.ds(hi - DEPTH, DEPTH - 1)], V0.at[:, pl.ds(0, DEPTH - 1)], down),
        edge(7, V0.at[:, hi - 1], V0.at[:, DEPTH - 1], down),
    ]

    def start(i):
        @pl.when(has_up)
        def _():
            to_up[i].start()

        @pl.when(has_down)
        def _():
            to_down[i].start()

    def arrived(i):
        @pl.when(has_up)
        def _():
            to_down[i].wait_recv()

        @pl.when(has_down)
        def _():
            to_up[i].wait_recv()

    def left(i):
        @pl.when(has_up)
        def _():
            to_up[i].wait_send()

        @pl.when(has_down)
        def _():
            to_down[i].wait_send()

    pl.semaphore_wait(barrier, n - 1)
    start(0)
    start(1)

    @pl.when(jnp.logical_not(has_up))
    def _():
        S[:, 0] = jnp.zeros((2, waves, cols), jnp.float32)
        E[pl.ds(0, DEPTH)] = jnp.zeros((DEPTH, 1, cols), jnp.float32)
        V[0, :, pl.ds(0, DEPTH)] = jnp.zeros((2, DEPTH, waves, cols), jnp.float32)

    @pl.when(jnp.logical_not(has_down))
    def _():
        S[:, rows + 1] = jnp.zeros((2, waves, cols), jnp.float32)
        E[pl.ds(hi, DEPTH)] = jnp.zeros((DEPTH, 1, cols), jnp.float32)
        V[0, :, pl.ds(hi, DEPTH)] = jnp.zeros((2, DEPTH, waves, cols), jnp.float32)

    @pl.loop(0, blocks)
    def _(b):
        for c in range(2):
            F[c, :, :, at(b)] = jnp.swapaxes(f_in[c, :, :, at(b)], 0, 1)

    wid = [pml_in[0, i].astype(jnp.float32) for i in range(4)]
    span = rows + 2 * DEPTH
    row_id = lax.broadcasted_iota(jnp.int32, (span, LANES), 0) + (first - DEPTH)
    inside = jnp.logical_and(row_id >= 0, row_id <= total - 1)
    am, a0, ap = three_point(row_id.astype(jnp.float32), wid[0], wid[1], total)
    for i, x in enumerate((am, a0, ap)):
        for c in range(2):
            RC[2 * i + c] = jnp.where(inside, x[c], 0.0)
    RC[2] = jnp.where(inside, a0[0], 0.0) + (2.0 - SHIFT)
    for e, base in enumerate((0, cols - LANES)):
        col_id = (lax.broadcasted_iota(jnp.int32, (8, LANES), 1) + base).astype(jnp.float32)
        bm, b0, bp = three_point(col_id, wid[2], wid[3], cols)
        for i, x in enumerate((bm, b0, bp)):
            for c in range(2):
                CC[e, 2 * i + c] = x[c]
        CC[e, 2] = b0[0] - 2.0

    wave_row = lax.broadcasted_iota(jnp.int32, (waves, LANES), 0)
    k2 = jnp.zeros((waves, LANES), jnp.float32)
    for w in range(waves):
        k2 = jnp.where(wave_row == w, wave_in[0, w], k2)
    k2 = k2 * k2

    m = cell_in.shape[1]
    cells = cell_in[...]
    bits = cols.bit_length() - 1
    cell_rows = lax.shift_right_logical(cells, bits)
    cell_cols = jnp.bitwise_and(cells, cols - 1).astype(jnp.float32)
    rows_hot = (
        cell_rows == lax.broadcasted_iota(jnp.int32, (rows, m), 0) + first
    ).astype(jnp.float32)
    diag = lax.broadcasted_iota(jnp.int32, (m, m), 0) == lax.broadcasted_iota(jnp.int32, (m, m), 1)
    col_at = jnp.sum(
        jnp.where(diag, jnp.broadcast_to(cell_cols, (m, m)), 0.0), axis=1, keepdims=True
    ).astype(jnp.int32)
    cols_hot = (col_at == lax.broadcasted_iota(jnp.int32, (m, cols), 1)).astype(jnp.float32)
    counts = jnp.dot(rows_hot, cols_hot, preferred_element_type=jnp.float32)
    for r in range(rows):
        CN[r] = MONITOR_GAIN * counts[r : r + 1]

    lane = lax.broadcasted_iota(jnp.int32, (waves, LANES), 1)
    is_first, is_last = lane == 0, lane == LANES - 1

    def shifted_image(src, t, r, emit):
        co = [
            jnp.broadcast_to(RC[i, pl.ds(r, 1), :], (waves, LANES)) for i in range(6)
        ]
        rolled = {}

        def get(b):
            if b not in rolled:
                x = [src[c, t, :, pl.ds(b * LANES, LANES)] for c in range(2)]
                rolled[b] = (
                    x,
                    [pltpu.roll(y, 1, 1) for y in x],
                    [pltpu.roll(y, LANES - 1, 1) for y in x],
                )
            return rolled[b]

        for b in range(blocks):
            here = pl.ds(b * LANES, LANES)
            v, r_left, r_right = get(b)
            before = get(b - 1)[1] if b > 0 else (0.0, 0.0)
            after = get(b + 1)[2] if b + 1 < blocks else (0.0, 0.0)
            lf = [jnp.where(is_first, before[c], r_left[c]) for c in range(2)]
            rt = [jnp.where(is_last, after[c], r_right[c]) for c in range(2)]
            above = [src[c, t - 1, :, here] for c in range(2)]
            below = [src[c, t + 1, :, here] for c in range(2)]
            mass = k2 * E[r, :, here]
            d = (co[2] - mass, co[3])
            if b == 0 or b == blocks - 1:
                e = 0 if b == 0 else 1
                cc = [CC[e, i] for i in range(6)]
                d = (d[0] + cc[2], d[1] + cc[3])
                side = cadd(cmul((cc[0], cc[1]), lf), cmul((cc[4], cc[5]), rt))
            else:
                side = cadd(lf, rt)
            out = csub(
                csub(cmul(d, v), side),
                cadd(cmul((co[0], co[1]), above), cmul((co[4], co[5]), below)),
            )
            emit(b, here, v, out)
            rolled.pop(b - 1, None)

    def residual_row(r):
        def emit(b, here, v, out):
            gain = CN[r, :, here]
            V[0, 0, DEPTH + r, :, here] = -gain * F[0, r, :, here] - (out[0] + SHIFT * v[0])
            V[0, 1, DEPTH + r, :, here] = gain * F[1, r, :, here] - (out[1] + SHIFT * v[1])

        shifted_image(S, r + 1, DEPTH + r, emit)

    def raise_row(k, r):
        def emit(b, here, v, out):
            V[k + 1, 0, r, :, here] = out[0]
            V[k + 1, 1, r, :, here] = out[1]

        shifted_image(V.at[k], r, r, emit)

    @pl.loop(1, rows - 1)
    def _(r):
        residual_row(r)

    start(2)
    arrived(0)

    @pl.loop(0, 2)
    def _(i):
        residual_row(i * (rows - 1))

    start(3)
    arrived(1)

    for k in range(DEPTH - 1):
        @pl.loop(lo + 1 + k, hi - 1 - k)
        def _(r):
            raise_row(k, r)

    arrived(2)
    arrived(3)

    for k in range(DEPTH):
        inner_lo, inner_hi = lo + 1 + k, hi - 1 - k
        outer_lo, outer_hi = 1 + k, span - 1 - k
        each = inner_lo - outer_lo
        gap = max(inner_hi - inner_lo, 0)

        @pl.loop(0, 2 * each)
        def _(i):
            raise_row(k, outer_lo + i + (i // each) * gap)

    pairs = [(i, j) for i in range(BASIS) for j in range(i, BASIS)]

    def gram_row(r, acc):
        acc = list(acc)
        for b in range(blocks):
            here = pl.ds(b * LANES, LANES)
            x = [[V[k, c, r, :, here] for c in range(2)] for k in range(BASIS)]
            slot = 0
            for i, j in pairs:
                a, z = x[i], x[j]
                acc[slot] = acc[slot] + (a[0] * z[0] + a[1] * z[1])
                slot += 1
                if i != j:
                    acc[slot] = acc[slot] + (a[0] * z[1] - a[1] * z[0])
                    slot += 1
        return tuple(acc)

    count = BASIS * BASIS
    zero = jnp.zeros((waves, LANES), jnp.float32)
    acc = lax.fori_loop(lo, hi, gram_row, (zero,) * count)
    packed = zero
    for i in range(count):
        packed = jnp.where(lane == i, jnp.sum(acc[i], axis=1, keepdims=True), packed)
    part_out[...] = packed
    part_in[me] = packed

    def sum_copy(d, target):
        return pltpu.make_async_remote_copy(
            src_ref=part_out, dst_ref=part_in.at[me], send_sem=sum_send.at[d],
            recv_sem=sum_recv.at[me], device_id=(part, target), device_id_type=MESH,
        )

    def sum_arrival(source):
        return pltpu.make_async_remote_copy(
            src_ref=part_out, dst_ref=part_in.at[source], send_sem=sum_send.at[0],
            recv_sem=sum_recv.at[source], device_id=(part, source), device_id_type=MESH,
        )

    @pl.loop(1, n)
    def _(d):
        sum_copy(d, lax.rem(me + d, n)).start()

    for i in range(DEPTH):
        left(i)

    @pl.loop(1, n)
    def _(d):
        sum_arrival(lax.rem(me + d, n)).wait_recv()

    @pl.loop(1, n)
    def _(d):
        sum_copy(d, lax.rem(me + d, n)).wait_send()

    whole = part_in[0]
    for i in range(1, n):
        whole = whole + part_in[i]
    gram, slot = {}, 0
    for i, j in pairs:
        re = jnp.broadcast_to(whole[:, slot : slot + 1], (waves, LANES))
        slot += 1
        im = zero
        if i != j:
            im = jnp.broadcast_to(whole[:, slot : slot + 1], (waves, LANES))
            slot += 1
        gram[(i, j)] = (re, im)
    weights = krylov_weights(gram, zero + 1.0, zero)
    k2m = -2.0 * k2

    for b in range(blocks):
        here = pl.ds(b * LANES, LANES)
        sol, grad = ([], []), []
        for r in range(rows):
            x = (S[0, r + 1, :, here], S[1, r + 1, :, here])
            for k, wk in enumerate(weights):
                x = cadd(x, cmul(wk, (V[k, 0, lo + r, :, here], V[k, 1, lo + r, :, here])))
            sol[0].append(x[0])
            sol[1].append(x[1])
            g = k2m * (x[0] * F[0, r, :, here] - x[1] * F[1, r, :, here])
            grad.append(jnp.sum(g, axis=0, keepdims=True))
        for c in range(2):
            adj_out[c, :, :, here] = jnp.swapaxes(jnp.stack(sol[c]), 0, 1)
        tile = jnp.concatenate(grad, axis=0)
        for q in range(LANES // width):
            tiles[b * (LANES // width) + q] = tile[:, q * width : (q + 1) * width]

    @pl.loop(0, n)
    def _(o):
        def pick(k, acc):
            return jnp.where(owner_in[0, k] == o, tiles[k], acc)

        ordered[o] = lax.fori_loop(0, n, pick, jnp.zeros((rows, width), jnp.float32), unroll=True)

    def tile_copy(d, target):
        return pltpu.make_async_remote_copy(
            src_ref=ordered.at[target], dst_ref=tiles_in.at[me], send_sem=tile_send.at[d],
            recv_sem=tile_recv.at[me], device_id=(part, target), device_id_type=MESH,
        )

    def tile_arrival(source):
        return pltpu.make_async_remote_copy(
            src_ref=ordered.at[source], dst_ref=tiles_in.at[source], send_sem=tile_send.at[0],
            recv_sem=tile_recv.at[source], device_id=(part, source), device_id_type=MESH,
        )

    @pl.loop(1, n)
    def _(d):
        tile_copy(d, lax.rem(me + d, n)).start()

    tiles_in[me] = ordered[me]

    @pl.loop(1, n)
    def _(d):
        tile_arrival(lax.rem(me + d, n)).wait_recv()

    @pl.loop(1, n)
    def _(d):
        tile_copy(d, lax.rem(me + d, n)).wait_send()

    for r in range(rows):
        grad_out[0, :, r * width : (r + 1) * width] = tiles_in[:, r, :]


def local(
    forward_field, adjoint_start, permittivity, wavenumbers, monitor_cells, pml_widths, owner_map
):
    n = lax.axis_size("space")
    _, waves, rows, cols = adjoint_start.shape
    width = cols // n
    span = rows + 2 * DEPTH
    f32 = jnp.float32
    vmem = pl.BlockSpec(memory_space=pltpu.VMEM)
    smem = pl.BlockSpec(memory_space=pltpu.SMEM)
    dma = pltpu.SemaphoreType.DMA
    return pl.pallas_call(
        functools.partial(kernel, n),
        out_shape=(
            jax.ShapeDtypeStruct(adjoint_start.shape, f32),
            jax.ShapeDtypeStruct((1, n, rows * width), f32),
        ),
        in_specs=[vmem, vmem, vmem, smem, vmem, smem, smem],
        out_specs=(vmem, vmem),
        scratch_shapes=[
            pltpu.VMEM((2, rows + 2, waves, cols), f32),
            pltpu.VMEM((2, rows, waves, cols), f32),
            pltpu.VMEM((BASIS, 2, span, waves, cols), f32),
            pltpu.VMEM((span, 1, cols), f32),
            pltpu.VMEM((rows, 1, cols), f32),
            pltpu.VMEM((6, span, LANES), f32),
            pltpu.VMEM((2, 6, 8, LANES), f32),
            pltpu.VMEM((waves, LANES), f32),
            pltpu.VMEM((n, waves, LANES), f32),
            pltpu.VMEM((n, rows, width), f32),
            pltpu.VMEM((n, rows, width), f32),
            pltpu.VMEM((n, rows, width), f32),
            dma((8,)),
            dma((8,)),
            dma((n,)),
            dma((n,)),
            dma((n,)),
            dma((n,)),
        ],
        compiler_params=pltpu.CompilerParams(
            collective_id=0, has_side_effects=True, vmem_limit_bytes=40 * 1024 * 1024
        ),
    )(
        forward_field,
        adjoint_start,
        permittivity,
        wavenumbers.reshape(1, -1),
        monitor_cells.reshape(1, -1),
        pml_widths.reshape(1, -1),
        owner_map,
    )


def solution(mesh):
    placed = (
        P(None, "parts", "space", None),
        P(None, "parts", "space", None),
        P(("parts", "space"), None),
        P("parts"),
        P("parts"),
        P("parts"),
        P(("parts", "space"), None),
    )
    return jax.shard_map(
        local,
        mesh=mesh,
        in_specs=placed,
        out_specs=(P(None, "parts", "space", None), P(("parts", "space"), None, None)),
        check_vma=False,
    )
```

```python
import functools

import jax
import jax.numpy as jnp
from jax import lax
from jax.experimental import pallas as pl
from jax.experimental.pallas import tpu as pltpu
from jax.sharding import PartitionSpec as P

ITERS = 2
SIGMA_PEAK = 4.0
MONITOR_GAIN = 4.0
SHIFT = 4.0
LANES = 128
DEPTH = 4
BASIS = 5
MESH = pl.DeviceIdType.MESH


def stretch(coord, low_width, high_width, total):
    lower_part = jnp.maximum(low_width - coord, 0.0) / low_width
    upper_part = jnp.maximum(coord - (total - 1.0 - high_width), 0.0) / high_width
    damping = SIGMA_PEAK * (
        lower_part * lower_part * lower_part + upper_part * upper_part * upper_part
    )
    denominator = 1.0 + damping * damping
    return (1.0 / denominator, -damping / denominator)


def cmul(a, b):
    return (a[0] * b[0] - a[1] * b[1], a[0] * b[1] + a[1] * b[0])


def cadd(a, b):
    return (a[0] + b[0], a[1] + b[1])


def csub(a, b):
    return (a[0] - b[0], a[1] - b[1])


def cdiv(top, bottom):
    d = bottom[0] * bottom[0] + bottom[1] * bottom[1]
    return (
        (top[0] * bottom[0] + top[1] * bottom[1]) / d,
        (top[1] * bottom[0] - top[0] * bottom[1]) / d,
    )


def three_point(coord, low, high, total):
    below = stretch(coord - 1.0, low, high, total)
    here = stretch(coord, low, high, total)
    above = stretch(coord + 1.0, low, high, total)
    face_low = stretch(coord - 0.5, low, high, total)
    face_high = stretch(coord + 0.5, low, high, total)
    return (
        cmul(face_low, below),
        cmul(cadd(face_low, face_high), here),
        cmul(face_high, above),
    )


def poly_dot(left, right, gram):
    total = None
    for i, a in enumerate(left):
        for j, b in enumerate(right):
            if i <= j:
                g = gram[(i, j)]
            else:
                g = (gram[(j, i)][0], -gram[(j, i)][1])
            term = cmul(cmul((a[0], -a[1]), b), g)
            total = term if total is None else cadd(total, term)
    return total


def poly_energy(q, gram):
    total = None
    for i, a in enumerate(q):
        term = (a[0] * a[0] + a[1] * a[1]) * gram[(i, i)][0]
        total = term if total is None else total + term
        for j in range(i + 1, len(q)):
            b = q[j]
            c_re = a[0] * b[0] + a[1] * b[1]
            c_im = a[0] * b[1] - a[1] * b[0]
            g = gram[(i, j)]
            total = total + 2.0 * (c_re * g[0] - c_im * g[1])
    return total


def poly_scale(c, p):
    return [cmul(c, a) for a in p]


def poly_add(p, q):
    out = []
    for i in range(max(len(p), len(q))):
        if i >= len(p):
            out.append(q[i])
        elif i >= len(q):
            out.append(p[i])
        else:
            out.append(cadd(p[i], q[i]))
    return out


def poly_sub(p, q):
    return poly_add(p, [(-a[0], -a[1]) for a in q])


def poly_image(p):
    raised = [None] + list(p)
    out = []
    for i in range(len(p) + 1):
        if i == 0:
            out.append((SHIFT * p[0][0], SHIFT * p[0][1]))
        elif i == len(p):
            out.append(raised[i])
        else:
            out.append((raised[i][0] + SHIFT * p[i][0], raised[i][1] + SHIFT * p[i][1]))
    return out


def krylov_weights(gram, one, zero):
    unit = (one, zero)
    residual = [unit]
    image = poly_image(residual)
    update = None
    quasi, first_dir, search = residual, residual, image
    direction = None
    start_sq = gram[(0, 0)][0]
    tau = jnp.sqrt(start_sq)
    theta, eta = zero, (zero, zero)
    rho = (start_sq, zero)

    def advance(norm_sq, tau, theta, eta, step, direction, guide, update):
        if direction is None:
            direction = guide
        else:
            ratio = cdiv(eta, step)
            coef = (theta * theta * ratio[0], theta * theta * ratio[1])
            direction = poly_add(guide, poly_scale(coef, direction))
        theta = jnp.sqrt(norm_sq) / tau
        shrink = 1.0 / (1.0 + theta * theta)
        tau = tau * theta * jnp.sqrt(shrink)
        eta = (shrink * step[0], shrink * step[1])
        move = poly_scale(eta, direction)
        update = move if update is None else poly_add(update, move)
        return direction, tau, theta, eta, update

    for iteration in range(ITERS):
        step = cdiv(rho, poly_dot(residual, search, gram))
        quasi = poly_sub(quasi, poly_scale(step, image))
        norm_sq = jnp.maximum(poly_energy(quasi, gram), 0.0)
        direction, tau, theta, eta, update = advance(
            norm_sq, tau, theta, eta, step, direction, first_dir, update
        )
        second_dir = poly_sub(first_dir, poly_scale(step, search))
        second_image = poly_image(second_dir)
        quasi = poly_sub(quasi, poly_scale(step, second_image))
        norm_sq = jnp.maximum(poly_energy(quasi, gram), 0.0)
        direction, tau, theta, eta, update = advance(
            norm_sq, tau, theta, eta, step, direction, second_dir, update
        )
        if iteration + 1 < ITERS:
            rho_new = poly_dot(residual, quasi, gram)
            beta = cdiv(rho_new, rho)
            rho = rho_new
            first_dir = poly_add(quasi, poly_scale(beta, second_dir))
            image = poly_image(first_dir)
            search = poly_add(
                image, poly_scale(beta, poly_add(second_image, poly_scale(beta, search)))
            )
    return update


def kernel(
    n, f_hbm, s_hbm, eps_hbm, wave_in, cell_in, pml_in, owner_in, adj_out, grad_out,
    f_in, s_in, eps_in, S, F, V, E, CN, RC, CC, part_out, part_in, tiles, ordered, tiles_in,
    tile_of, load_sem, edge_send, edge_recv, sum_send, sum_recv, tile_send, tile_recv,
):
    waves, rows, cols = s_in.shape[1], s_in.shape[2], s_in.shape[3]
    blocks = cols // LANES
    width = cols // n
    me = lax.axis_index("space")
    part = lax.axis_index("parts")
    first = me * rows
    total = rows * n
    up, down = me - 1, me + 1
    has_up, has_down = me > 0, me < n - 1

    load_f = pltpu.make_async_copy(f_hbm, f_in, load_sem.at[0])
    load_eps = pltpu.make_async_copy(eps_hbm, eps_in, load_sem.at[1])
    load_s = [pltpu.make_async_copy(s_hbm.at[c], s_in.at[c], load_sem.at[2 + c]) for c in range(2)]
    load_s[0].start()
    load_s[1].start()
    load_eps.start()
    load_f.start()

    barrier = pltpu.get_barrier_semaphore()

    @pl.loop(1, n)
    def _(d):
        pl.semaphore_signal(
            barrier, inc=1, device_id=(part, lax.rem(me + d, n)), device_id_type=MESH
        )

    def at(b):
        return pl.ds(pl.multiple_of(b * LANES, LANES), LANES)

    for c in range(2):
        load_s[c].wait()

        @pl.loop(0, blocks)
        def _(b):
            S[c, pl.ds(1, rows), :, at(b)] = jnp.swapaxes(s_in[c, :, :, at(b)], 0, 1)

    def edge(slot, src, dst, target):
        return pltpu.make_async_remote_copy(
            src_ref=src, dst_ref=dst, send_sem=edge_send.at[slot], recv_sem=edge_recv.at[slot],
            device_id=(part, target), device_id_type=MESH,
        )

    V0 = V.at[0]
    lo, hi = DEPTH, DEPTH + rows
    reach = DEPTH - 1
    slots = DEPTH + 2

    def to_up(i):
        if isinstance(i, int) and i == 0:
            return edge(0, S.at[:, 1], S.at[:, rows + 1], up)
        if isinstance(i, int) and i == 1:
            return edge(1, E.at[pl.ds(lo, reach)], E.at[pl.ds(hi, reach)], up)
        return edge(i, V0.at[:, lo + i - 2], V0.at[:, hi + i - 2], up)

    def to_down(i):
        if isinstance(i, int) and i == 0:
            return edge(slots, S.at[:, rows], S.at[:, 0], down)
        if isinstance(i, int) and i == 1:
            return edge(
                slots + 1, E.at[pl.ds(hi - reach, reach)], E.at[pl.ds(lo - reach, reach)], down
            )
        return edge(slots + i, V0.at[:, hi + 1 - i], V0.at[:, lo + 1 - i], down)

    def start(i):
        @pl.when(has_up)
        def _():
            to_up(i).start()

        @pl.when(has_down)
        def _():
            to_down(i).start()

    def arrived(i):
        @pl.when(has_up)
        def _():
            to_down(i).wait_recv()

        @pl.when(has_down)
        def _():
            to_up(i).wait_recv()

    def left(i):
        @pl.when(has_up)
        def _():
            to_up(i).wait_send()

        @pl.when(has_down)
        def _():
            to_down(i).wait_send()

    pl.semaphore_wait(barrier, n - 1)
    start(0)

    @pl.when(jnp.logical_not(has_up))
    def _():
        S[:, 0] = jnp.zeros((2, waves, cols), jnp.float32)
        E[pl.ds(0, DEPTH)] = jnp.zeros((DEPTH, 1, cols), jnp.float32)
        V[0, :, pl.ds(0, DEPTH)] = jnp.zeros((2, DEPTH, waves, cols), jnp.float32)

    @pl.when(jnp.logical_not(has_down))
    def _():
        S[:, rows + 1] = jnp.zeros((2, waves, cols), jnp.float32)
        E[pl.ds(hi, DEPTH)] = jnp.zeros((DEPTH, 1, cols), jnp.float32)
        V[0, :, pl.ds(hi, DEPTH)] = jnp.zeros((2, DEPTH, waves, cols), jnp.float32)

    load_eps.wait()
    for r in range(rows):
        E[DEPTH + r] = eps_in[pl.ds(r, 1), :]
    start(1)

    load_f.wait()

    @pl.loop(0, blocks)
    def _(b):
        for c in range(2):
            F[c, :, :, at(b)] = jnp.swapaxes(f_in[c, :, :, at(b)], 0, 1)

    wid = [pml_in[0, i].astype(jnp.float32) for i in range(4)]
    span = rows + 2 * DEPTH
    row_id = lax.broadcasted_iota(jnp.int32, (span, LANES), 0) + (first - DEPTH)
    inside = jnp.logical_and(row_id >= 0, row_id <= total - 1)
    am, a0, ap = three_point(row_id.astype(jnp.float32), wid[0], wid[1], total)
    for i, x in enumerate((am, a0, ap)):
        for c in range(2):
            RC[2 * i + c] = jnp.where(inside, x[c], 0.0)
    RC[2] = jnp.where(inside, a0[0], 0.0) + (2.0 - SHIFT)
    for e, base in enumerate((0, cols - LANES)):
        col_id = (lax.broadcasted_iota(jnp.int32, (8, LANES), 1) + base).astype(jnp.float32)
        bm, b0, bp = three_point(col_id, wid[2], wid[3], cols)
        for i, x in enumerate((bm, b0, bp)):
            for c in range(2):
                CC[e, 2 * i + c] = x[c]
        CC[e, 2] = b0[0] - 2.0

    wave_row = lax.broadcasted_iota(jnp.int32, (waves, LANES), 0)
    k2 = jnp.zeros((waves, LANES), jnp.float32)
    for w in range(waves):
        k2 = jnp.where(wave_row == w, wave_in[0, w], k2)
    k2 = k2 * k2

    m = cell_in.shape[1]
    cells = cell_in[...]
    bits = cols.bit_length() - 1
    cell_rows = lax.shift_right_logical(cells, bits)
    cell_cols = jnp.bitwise_and(cells, cols - 1).astype(jnp.float32)
    rows_hot = (
        cell_rows == lax.broadcasted_iota(jnp.int32, (rows, m), 0) + first
    ).astype(jnp.float32)
    diag = lax.broadcasted_iota(jnp.int32, (m, m), 0) == lax.broadcasted_iota(jnp.int32, (m, m), 1)
    col_at = jnp.sum(
        jnp.where(diag, jnp.broadcast_to(cell_cols, (m, m)), 0.0), axis=1, keepdims=True
    ).astype(jnp.int32)
    cols_hot = (col_at == lax.broadcasted_iota(jnp.int32, (m, cols), 1)).astype(jnp.float32)
    counts = jnp.dot(rows_hot, cols_hot, preferred_element_type=jnp.float32)
    for r in range(rows):
        CN[r] = MONITOR_GAIN * counts[r : r + 1]

    lane = lax.broadcasted_iota(jnp.int32, (waves, LANES), 1)
    is_first, is_last = lane == 0, lane == LANES - 1

    def shifted_image(src, t, r, emit):
        co = [
            jnp.broadcast_to(RC[i, pl.ds(r, 1), :], (waves, LANES)) for i in range(6)
        ]
        rolled = {}

        def get(b):
            if b not in rolled:
                x = [src[c, t, :, pl.ds(b * LANES, LANES)] for c in range(2)]
                rolled[b] = (
                    x,
                    [pltpu.roll(y, 1, 1) for y in x],
                    [pltpu.roll(y, LANES - 1, 1) for y in x],
                )
            return rolled[b]

        for b in range(blocks):
            here = pl.ds(b * LANES, LANES)
            v, r_left, r_right = get(b)
            before = get(b - 1)[1] if b > 0 else (0.0, 0.0)
            after = get(b + 1)[2] if b + 1 < blocks else (0.0, 0.0)
            lf = [jnp.where(is_first, before[c], r_left[c]) for c in range(2)]
            rt = [jnp.where(is_last, after[c], r_right[c]) for c in range(2)]
            above = [src[c, t - 1, :, here] for c in range(2)]
            below = [src[c, t + 1, :, here] for c in range(2)]
            mass = k2 * E[r, :, here]
            d = (co[2] - mass, co[3])
            if b == 0 or b == blocks - 1:
                e = 0 if b == 0 else 1
                cc = [CC[e, i] for i in range(6)]
                d = (d[0] + cc[2], d[1] + cc[3])
                side = cadd(cmul((cc[0], cc[1]), lf), cmul((cc[4], cc[5]), rt))
            else:
                side = cadd(lf, rt)
            out = csub(
                csub(cmul(d, v), side),
                cadd(cmul((co[0], co[1]), above), cmul((co[4], co[5]), below)),
            )
            emit(b, here, v, out)
            rolled.pop(b - 1, None)

    def residual_row(r):
        def emit(b, here, v, out):
            gain = CN[r, :, here]
            V[0, 0, DEPTH + r, :, here] = -gain * F[0, r, :, here] - (out[0] + SHIFT * v[0])
            V[0, 1, DEPTH + r, :, here] = gain * F[1, r, :, here] - (out[1] + SHIFT * v[1])

        shifted_image(S, r + 1, DEPTH + r, emit)

    def raise_row(k, r):
        def emit(b, here, v, out):
            V[k + 1, 0, r, :, here] = out[0]
            V[k + 1, 1, r, :, here] = out[1]

        shifted_image(V.at[k], r, r, emit)

    @pl.loop(0, 2)
    def _(i):
        residual_row(1 + i * (rows - 3))

    start(3)

    @pl.loop(2, rows - 2)
    def _(r):
        residual_row(r)

    arrived(0)

    @pl.loop(0, 2)
    def _(i):
        residual_row(i * (rows - 1))

    start(2)
    start(4)
    start(5)

    @pl.loop(0, n)
    def _(o):
        def count(k, found):
            return jnp.where(owner_in[0, k] == o, k, found)

        tile_of[o] = lax.fori_loop(0, n, count, jnp.int32(0), unroll=True)

    for k in range(DEPTH - 1):
        @pl.loop(lo + 1 + k, hi - 1 - k)
        def _(r):
            raise_row(k, r)

    arrived(1)

    pairs = [(i, j) for i in range(BASIS) for j in range(i, BASIS)]

    def gram_row(r, acc):
        acc = list(acc)
        for b in range(blocks):
            here = pl.ds(b * LANES, LANES)
            x = [[V[k, c, r, :, here] for c in range(2)] for k in range(BASIS)]
            slot = 0
            for i, j in pairs:
                a, z = x[i], x[j]
                acc[slot] = acc[slot] + (a[0] * z[0] + a[1] * z[1])
                slot += 1
                if i != j:
                    acc[slot] = acc[slot] + (a[0] * z[1] - a[1] * z[0])
                    slot += 1
        return tuple(acc)

    count = BASIS * BASIS
    zero = jnp.zeros((waves, LANES), jnp.float32)

    def stage(j, acc):
        arrived(1 + j)

        @pl.loop(0, 2 * DEPTH)
        def _(i):
            k = i // 2
            d = j - 1 - k
            raise_row(k, lo - d + lax.rem(i, 2) * (rows - 1 + 2 * d))

        def near(i, acc):
            d = DEPTH - j
            return gram_row(lo + d + i * (rows - 1 - 2 * d), acc)

        return lax.fori_loop(0, 2, near, acc)

    acc = lax.fori_loop(1, DEPTH + 1, stage, (zero,) * count)
    packed = zero
    for i in range(count):
        packed = jnp.where(lane == i, jnp.sum(acc[i], axis=1, keepdims=True), packed)
    group = LANES // 32
    spread = zero
    for g in range(group):
        moved = packed if g == 0 else pltpu.roll(packed, 32 * g, 1)
        spread = jnp.where(lax.rem(wave_row, group) == g, moved, spread)
    for q in range(waves // group):
        mine = jnp.logical_and(wave_row >= q * group, wave_row < (q + 1) * group)
        part_out[q : q + 1, :] = jnp.sum(jnp.where(mine, spread, 0.0), axis=0, keepdims=True)
    part_in[me] = part_out[...]

    def sum_copy(d, target):
        return pltpu.make_async_remote_copy(
            src_ref=part_out, dst_ref=part_in.at[me], send_sem=sum_send.at[d],
            recv_sem=sum_recv.at[me], device_id=(part, target), device_id_type=MESH,
        )

    def sum_arrival(source):
        return pltpu.make_async_remote_copy(
            src_ref=part_out, dst_ref=part_in.at[source], send_sem=sum_send.at[0],
            recv_sem=sum_recv.at[source], device_id=(part, source), device_id_type=MESH,
        )

    @pl.loop(1, n)
    def _(d):
        sum_copy(d, lax.rem(me + d, n)).start()

    for i in range(slots):
        left(i)

    @pl.loop(1, n)
    def _(d):
        sum_arrival(lax.rem(me + d, n)).wait_recv()

    summed = part_in[0]
    for i in range(1, n):
        summed = summed + part_in[i]
    whole = zero
    for w in range(waves):
        row = jnp.broadcast_to(summed[w // group : w // group + 1, :], (waves, LANES))
        back = (LANES - 32 * (w % group)) % LANES
        whole = jnp.where(wave_row == w, pltpu.roll(row, back, 1) if back else row, whole)
    gram, slot = {}, 0
    for i, j in pairs:
        re = jnp.broadcast_to(whole[:, slot : slot + 1], (waves, LANES))
        slot += 1
        im = zero
        if i != j:
            im = jnp.broadcast_to(whole[:, slot : slot + 1], (waves, LANES))
            slot += 1
        gram[(i, j)] = (re, im)
    weights = krylov_weights(gram, zero + 1.0, zero)
    k2m = -2.0 * k2

    for b in range(blocks):
        here = pl.ds(b * LANES, LANES)
        grad = []
        for r in range(rows):
            x = (S[0, r + 1, :, here], S[1, r + 1, :, here])
            for k, wk in enumerate(weights):
                x = cadd(x, cmul(wk, (V[k, 0, lo + r, :, here], V[k, 1, lo + r, :, here])))
            V[0, 0, lo + r, :, here] = x[0]
            V[0, 1, lo + r, :, here] = x[1]
            g = k2m * (x[0] * F[0, r, :, here] - x[1] * F[1, r, :, here])
            grad.append(jnp.sum(g, axis=0, keepdims=True))
        tile = jnp.concatenate(grad, axis=0)
        for q in range(LANES // width):
            tiles[b * (LANES // width) + q] = tile[:, q * width : (q + 1) * width]

    for o in range(n):
        ordered[o] = tiles[tile_of[o]]

    def tile_copy(d, target):
        return pltpu.make_async_remote_copy(
            src_ref=ordered.at[target], dst_ref=tiles_in.at[me], send_sem=tile_send.at[d],
            recv_sem=tile_recv.at[me], device_id=(part, target), device_id_type=MESH,
        )

    def tile_arrival(source):
        return pltpu.make_async_remote_copy(
            src_ref=ordered.at[source], dst_ref=tiles_in.at[source], send_sem=tile_send.at[0],
            recv_sem=tile_recv.at[source], device_id=(part, source), device_id_type=MESH,
        )

    @pl.loop(1, n)
    def _(d):
        tile_copy(d, lax.rem(me + d, n)).start()

    tiles_in[me] = ordered[me]

    @pl.loop(0, blocks)
    def _(b):
        for c in range(2):
            adj_out[c, :, :, at(b)] = jnp.swapaxes(V[0, c, pl.ds(lo, rows), :, at(b)], 0, 1)

    @pl.loop(1, n)
    def _(d):
        sum_copy(d, lax.rem(me + d, n)).wait_send()

    @pl.loop(1, n)
    def _(d):
        tile_arrival(lax.rem(me + d, n)).wait_recv()

    @pl.loop(1, n)
    def _(d):
        tile_copy(d, lax.rem(me + d, n)).wait_send()

    for r in range(rows):
        grad_out[0, :, r * width : (r + 1) * width] = tiles_in[:, r, :]


def local(
    forward_field, adjoint_start, permittivity, wavenumbers, monitor_cells, pml_widths, owner_map
):
    n = lax.axis_size("space")
    _, waves, rows, cols = adjoint_start.shape
    width = cols // n
    span = rows + 2 * DEPTH
    f32 = jnp.float32
    vmem = pl.BlockSpec(memory_space=pltpu.VMEM)
    smem = pl.BlockSpec(memory_space=pltpu.SMEM)
    hbm = pl.BlockSpec(memory_space=pltpu.HBM)
    dma = pltpu.SemaphoreType.DMA
    return pl.pallas_call(
        functools.partial(kernel, n),
        out_shape=(
            jax.ShapeDtypeStruct(adjoint_start.shape, f32),
            jax.ShapeDtypeStruct((1, n, rows * width), f32),
        ),
        in_specs=[hbm, hbm, hbm, smem, vmem, smem, smem],
        out_specs=(vmem, vmem),
        scratch_shapes=[
            pltpu.VMEM((2, waves, rows, cols), f32),
            pltpu.VMEM((2, waves, rows, cols), f32),
            pltpu.VMEM((rows, cols), f32),
            pltpu.VMEM((2, rows + 2, waves, cols), f32),
            pltpu.VMEM((2, rows, waves, cols), f32),
            pltpu.VMEM((BASIS, 2, span, waves, cols), f32),
            pltpu.VMEM((span, 1, cols), f32),
            pltpu.VMEM((rows, 1, cols), f32),
            pltpu.VMEM((6, span, LANES), f32),
            pltpu.VMEM((2, 6, 8, LANES), f32),
            pltpu.VMEM((waves * 32 // LANES, LANES), f32),
            pltpu.VMEM((n, waves * 32 // LANES, LANES), f32),
            pltpu.VMEM((n, rows, width), f32),
            pltpu.VMEM((n, rows, width), f32),
            pltpu.VMEM((n, rows, width), f32),
            pltpu.SMEM((n,), jnp.int32),
            dma((4,)),
            dma((2 * DEPTH + 4,)),
            dma((2 * DEPTH + 4,)),
            dma((n,)),
            dma((n,)),
            dma((n,)),
            dma((n,)),
        ],
        compiler_params=pltpu.CompilerParams(
            collective_id=0, has_side_effects=True, vmem_limit_bytes=40 * 1024 * 1024
        ),
    )(
        forward_field,
        adjoint_start,
        permittivity,
        wavenumbers.reshape(1, -1),
        monitor_cells.reshape(1, -1),
        pml_widths.reshape(1, -1),
        owner_map,
    )


def solution(mesh):
    placed = (
        P(None, "parts", "space", None),
        P(None, "parts", "space", None),
        P(("parts", "space"), None),
        P("parts"),
        P("parts"),
        P("parts"),
        P(("parts", "space"), None),
    )
    return jax.shard_map(
        local,
        mesh=mesh,
        in_specs=placed,
        out_specs=(P(None, "parts", "space", None), P(("parts", "space"), None, None)),
        check_vma=False,
    )
```

```python
import functools

import jax
import jax.numpy as jnp
from jax import lax
from jax.experimental import pallas as pl
from jax.experimental.pallas import tpu as pltpu
from jax.sharding import PartitionSpec as P

ITERS = 2
SIGMA_PEAK = 4.0
MONITOR_GAIN = 4.0
SHIFT = 4.0
LANES = 128
DEPTH = 4
BASIS = 5
MESH = pl.DeviceIdType.MESH


def stretch(coord, low_width, high_width, total):
    lower_part = jnp.maximum(low_width - coord, 0.0) / low_width
    upper_part = jnp.maximum(coord - (total - 1.0 - high_width), 0.0) / high_width
    damping = SIGMA_PEAK * (
        lower_part * lower_part * lower_part + upper_part * upper_part * upper_part
    )
    denominator = 1.0 + damping * damping
    return (1.0 / denominator, -damping / denominator)


def cmul(a, b):
    return (a[0] * b[0] - a[1] * b[1], a[0] * b[1] + a[1] * b[0])


def cadd(a, b):
    return (a[0] + b[0], a[1] + b[1])


def csub(a, b):
    return (a[0] - b[0], a[1] - b[1])


def cdiv(top, bottom):
    d = bottom[0] * bottom[0] + bottom[1] * bottom[1]
    return (
        (top[0] * bottom[0] + top[1] * bottom[1]) / d,
        (top[1] * bottom[0] - top[0] * bottom[1]) / d,
    )


def three_point(coord, low, high, total):
    below = stretch(coord - 1.0, low, high, total)
    here = stretch(coord, low, high, total)
    above = stretch(coord + 1.0, low, high, total)
    face_low = stretch(coord - 0.5, low, high, total)
    face_high = stretch(coord + 0.5, low, high, total)
    return (
        cmul(face_low, below),
        cmul(cadd(face_low, face_high), here),
        cmul(face_high, above),
    )


def poly_dot(left, right, gram):
    total = None
    for i, a in enumerate(left):
        for j, b in enumerate(right):
            if i <= j:
                g = gram[(i, j)]
            else:
                g = (gram[(j, i)][0], -gram[(j, i)][1])
            term = cmul(cmul((a[0], -a[1]), b), g)
            total = term if total is None else cadd(total, term)
    return total


def poly_energy(q, gram):
    total = None
    for i, a in enumerate(q):
        term = (a[0] * a[0] + a[1] * a[1]) * gram[(i, i)][0]
        total = term if total is None else total + term
        for j in range(i + 1, len(q)):
            b = q[j]
            c_re = a[0] * b[0] + a[1] * b[1]
            c_im = a[0] * b[1] - a[1] * b[0]
            g = gram[(i, j)]
            total = total + 2.0 * (c_re * g[0] - c_im * g[1])
    return total


def poly_scale(c, p):
    return [cmul(c, a) for a in p]


def poly_add(p, q):
    out = []
    for i in range(max(len(p), len(q))):
        if i >= len(p):
            out.append(q[i])
        elif i >= len(q):
            out.append(p[i])
        else:
            out.append(cadd(p[i], q[i]))
    return out


def poly_sub(p, q):
    return poly_add(p, [(-a[0], -a[1]) for a in q])


def poly_image(p):
    raised = [None] + list(p)
    out = []
    for i in range(len(p) + 1):
        if i == 0:
            out.append((SHIFT * p[0][0], SHIFT * p[0][1]))
        elif i == len(p):
            out.append(raised[i])
        else:
            out.append((raised[i][0] + SHIFT * p[i][0], raised[i][1] + SHIFT * p[i][1]))
    return out


def krylov_weights(gram, one, zero):
    unit = (one, zero)
    residual = [unit]
    image = poly_image(residual)
    update = None
    quasi, first_dir, search = residual, residual, image
    direction = None
    start_sq = gram[(0, 0)][0]
    tau = jnp.sqrt(start_sq)
    theta, eta = zero, (zero, zero)
    rho = (start_sq, zero)

    def advance(norm_sq, tau, theta, eta, step, direction, guide, update):
        if direction is None:
            direction = guide
        else:
            ratio = cdiv(eta, step)
            coef = (theta * theta * ratio[0], theta * theta * ratio[1])
            direction = poly_add(guide, poly_scale(coef, direction))
        theta = jnp.sqrt(norm_sq) / tau
        shrink = 1.0 / (1.0 + theta * theta)
        tau = tau * theta * jnp.sqrt(shrink)
        eta = (shrink * step[0], shrink * step[1])
        move = poly_scale(eta, direction)
        update = move if update is None else poly_add(update, move)
        return direction, tau, theta, eta, update

    for iteration in range(ITERS):
        step = cdiv(rho, poly_dot(residual, search, gram))
        quasi = poly_sub(quasi, poly_scale(step, image))
        norm_sq = jnp.maximum(poly_energy(quasi, gram), 0.0)
        direction, tau, theta, eta, update = advance(
            norm_sq, tau, theta, eta, step, direction, first_dir, update
        )
        second_dir = poly_sub(first_dir, poly_scale(step, search))
        second_image = poly_image(second_dir)
        quasi = poly_sub(quasi, poly_scale(step, second_image))
        norm_sq = jnp.maximum(poly_energy(quasi, gram), 0.0)
        direction, tau, theta, eta, update = advance(
            norm_sq, tau, theta, eta, step, direction, second_dir, update
        )
        if iteration + 1 < ITERS:
            rho_new = poly_dot(residual, quasi, gram)
            beta = cdiv(rho_new, rho)
            rho = rho_new
            first_dir = poly_add(quasi, poly_scale(beta, second_dir))
            image = poly_image(first_dir)
            search = poly_add(
                image, poly_scale(beta, poly_add(second_image, poly_scale(beta, search)))
            )
    return update


def kernel(
    n, f_hbm, s_hbm, eps_hbm, wave_in, cell_in, pml_in, owner_in, adj_out, grad_out,
    f_in, s_in, eps_in, S, F, V, E, CN, RC, CC, part_out, part_in, tiles, ordered, tiles_in,
    tile_of, load_sem, edge_send, edge_recv, sum_send, sum_recv, tile_send, tile_recv,
):
    waves, rows, cols = s_in.shape[1], s_in.shape[2], s_in.shape[3]
    blocks = cols // LANES
    width = cols // n
    me = lax.axis_index("space")
    part = lax.axis_index("parts")
    first = me * rows
    total = rows * n
    up, down = me - 1, me + 1
    has_up, has_down = me > 0, me < n - 1

    load_f = pltpu.make_async_copy(f_hbm, f_in, load_sem.at[0])
    load_eps = pltpu.make_async_copy(eps_hbm, eps_in, load_sem.at[1])
    load_s = [pltpu.make_async_copy(s_hbm.at[c], s_in.at[c], load_sem.at[2 + c]) for c in range(2)]
    load_s[0].start()
    load_s[1].start()
    load_eps.start()
    load_f.start()

    barrier = pltpu.get_barrier_semaphore()

    @pl.loop(1, n)
    def _(d):
        pl.semaphore_signal(
            barrier, inc=1, device_id=(part, lax.rem(me + d, n)), device_id_type=MESH
        )

    def at(b):
        return pl.ds(pl.multiple_of(b * LANES, LANES), LANES)

    for c in range(2):
        load_s[c].wait()

        @pl.loop(0, blocks)
        def _(b):
            S[c, pl.ds(1, rows), :, at(b)] = jnp.swapaxes(s_in[c, :, :, at(b)], 0, 1)

    def edge(slot, src, dst, target):
        return pltpu.make_async_remote_copy(
            src_ref=src, dst_ref=dst, send_sem=edge_send.at[slot], recv_sem=edge_recv.at[slot],
            device_id=(part, target), device_id_type=MESH,
        )

    V0 = V.at[0]
    lo, hi = DEPTH, DEPTH + rows
    reach = DEPTH - 1
    slots = DEPTH + 2

    def to_up(i):
        if isinstance(i, int) and i == 0:
            return edge(0, S.at[:, 1], S.at[:, rows + 1], up)
        if isinstance(i, int) and i == 1:
            return edge(1, E.at[pl.ds(lo, reach)], E.at[pl.ds(hi, reach)], up)
        return edge(i, V0.at[:, lo + i - 2], V0.at[:, hi + i - 2], up)

    def to_down(i):
        if isinstance(i, int) and i == 0:
            return edge(slots, S.at[:, rows], S.at[:, 0], down)
        if isinstance(i, int) and i == 1:
            return edge(
                slots + 1, E.at[pl.ds(hi - reach, reach)], E.at[pl.ds(lo - reach, reach)], down
            )
        return edge(slots + i, V0.at[:, hi + 1 - i], V0.at[:, lo + 1 - i], down)

    def start(i):
        @pl.when(has_up)
        def _():
            to_up(i).start()

        @pl.when(has_down)
        def _():
            to_down(i).start()

    def arrived(i):
        @pl.when(has_up)
        def _():
            to_down(i).wait_recv()

        @pl.when(has_down)
        def _():
            to_up(i).wait_recv()

    def left(i):
        @pl.when(has_up)
        def _():
            to_up(i).wait_send()

        @pl.when(has_down)
        def _():
            to_down(i).wait_send()

    pl.semaphore_wait(barrier, n - 1)
    start(0)

    @pl.when(jnp.logical_not(has_up))
    def _():
        S[:, 0] = jnp.zeros((2, waves, cols), jnp.float32)
        E[pl.ds(0, DEPTH)] = jnp.zeros((DEPTH, 1, cols), jnp.float32)
        V[0, :, pl.ds(0, DEPTH)] = jnp.zeros((2, DEPTH, waves, cols), jnp.float32)

    @pl.when(jnp.logical_not(has_down))
    def _():
        S[:, rows + 1] = jnp.zeros((2, waves, cols), jnp.float32)
        E[pl.ds(hi, DEPTH)] = jnp.zeros((DEPTH, 1, cols), jnp.float32)
        V[0, :, pl.ds(hi, DEPTH)] = jnp.zeros((2, DEPTH, waves, cols), jnp.float32)

    load_eps.wait()
    for r in range(rows):
        E[DEPTH + r] = eps_in[pl.ds(r, 1), :]
    start(1)

    load_f.wait()

    @pl.loop(0, blocks)
    def _(b):
        for c in range(2):
            F[c, :, :, at(b)] = jnp.swapaxes(f_in[c, :, :, at(b)], 0, 1)

    wid = [pml_in[0, i].astype(jnp.float32) for i in range(4)]
    span = rows + 2 * DEPTH
    row_id = lax.broadcasted_iota(jnp.int32, (span, LANES), 0) + (first - DEPTH)
    inside = jnp.logical_and(row_id >= 0, row_id <= total - 1)
    am, a0, ap = three_point(row_id.astype(jnp.float32), wid[0], wid[1], total)
    for i, x in enumerate((am, a0, ap)):
        for c in range(2):
            RC[2 * i + c] = jnp.where(inside, x[c], 0.0)
    RC[2] = jnp.where(inside, a0[0], 0.0) + (2.0 - SHIFT)
    for e, base in enumerate((0, cols - LANES)):
        col_id = (lax.broadcasted_iota(jnp.int32, (8, LANES), 1) + base).astype(jnp.float32)
        bm, b0, bp = three_point(col_id, wid[2], wid[3], cols)
        for i, x in enumerate((bm, b0, bp)):
            for c in range(2):
                CC[e, 2 * i + c] = x[c]
        CC[e, 2] = b0[0] - 2.0

    wave_row = lax.broadcasted_iota(jnp.int32, (waves, LANES), 0)
    k2 = jnp.zeros((waves, LANES), jnp.float32)
    for w in range(waves):
        k2 = jnp.where(wave_row == w, wave_in[0, w], k2)
    k2 = k2 * k2

    m = cell_in.shape[1]
    cells = cell_in[...]
    bits = cols.bit_length() - 1
    cell_rows = lax.shift_right_logical(cells, bits)
    cell_cols = jnp.bitwise_and(cells, cols - 1).astype(jnp.float32)
    rows_hot = (
        cell_rows == lax.broadcasted_iota(jnp.int32, (rows, m), 0) + first
    ).astype(jnp.float32)
    diag = lax.broadcasted_iota(jnp.int32, (m, m), 0) == lax.broadcasted_iota(jnp.int32, (m, m), 1)
    col_at = jnp.sum(
        jnp.where(diag, jnp.broadcast_to(cell_cols, (m, m)), 0.0), axis=1, keepdims=True
    ).astype(jnp.int32)
    cols_hot = (col_at == lax.broadcasted_iota(jnp.int32, (m, cols), 1)).astype(jnp.float32)
    counts = jnp.dot(rows_hot, cols_hot, preferred_element_type=jnp.float32)
    for r in range(rows):
        CN[r] = MONITOR_GAIN * counts[r : r + 1]

    lane = lax.broadcasted_iota(jnp.int32, (waves, LANES), 1)
    is_first, is_last = lane == 0, lane == LANES - 1

    def shifted_image(src, t, r, emit):
        co = [
            jnp.broadcast_to(RC[i, pl.ds(r, 1), :], (waves, LANES)) for i in range(6)
        ]
        rolled = {}

        def get(b):
            if b not in rolled:
                x = [src[c, t, :, pl.ds(b * LANES, LANES)] for c in range(2)]
                rolled[b] = (
                    x,
                    [pltpu.roll(y, 1, 1) for y in x],
                    [pltpu.roll(y, LANES - 1, 1) for y in x],
                )
            return rolled[b]

        for b in range(blocks):
            here = pl.ds(b * LANES, LANES)
            v, r_left, r_right = get(b)
            before = get(b - 1)[1] if b > 0 else (0.0, 0.0)
            after = get(b + 1)[2] if b + 1 < blocks else (0.0, 0.0)
            lf = [jnp.where(is_first, before[c], r_left[c]) for c in range(2)]
            rt = [jnp.where(is_last, after[c], r_right[c]) for c in range(2)]
            above = [src[c, t - 1, :, here] for c in range(2)]
            below = [src[c, t + 1, :, here] for c in range(2)]
            mass = k2 * E[r, :, here]
            d = (co[2] - mass, co[3])
            if b == 0 or b == blocks - 1:
                e = 0 if b == 0 else 1
                cc = [CC[e, i] for i in range(6)]
                d = (d[0] + cc[2], d[1] + cc[3])
                side = cadd(cmul((cc[0], cc[1]), lf), cmul((cc[4], cc[5]), rt))
            else:
                side = cadd(lf, rt)
            out = csub(
                csub(cmul(d, v), side),
                cadd(cmul((co[0], co[1]), above), cmul((co[4], co[5]), below)),
            )
            emit(b, here, v, out)
            rolled.pop(b - 1, None)

    def residual_row(r):
        def emit(b, here, v, out):
            gain = CN[r, :, here]
            V[0, 0, DEPTH + r, :, here] = -gain * F[0, r, :, here] - (out[0] + SHIFT * v[0])
            V[0, 1, DEPTH + r, :, here] = gain * F[1, r, :, here] - (out[1] + SHIFT * v[1])

        shifted_image(S, r + 1, DEPTH + r, emit)

    def raise_row(k, r):
        def emit(b, here, v, out):
            V[k + 1, 0, r, :, here] = out[0]
            V[k + 1, 1, r, :, here] = out[1]

        shifted_image(V.at[k], r, r, emit)

    @pl.loop(0, 2)
    def _(i):
        residual_row(1 + i * (rows - 3))

    @pl.loop(2, rows - 2)
    def _(r):
        residual_row(r)

    left(0)
    arrived(0)

    @pl.loop(0, 2)
    def _(i):
        residual_row(i * (rows - 1))

    start(2)
    start(3)

    @pl.loop(0, n)
    def _(o):
        def count(k, found):
            return jnp.where(owner_in[0, k] == o, k, found)

        tile_of[o] = lax.fori_loop(0, n, count, jnp.int32(0), unroll=True)

    for k in range(DEPTH - 1):
        @pl.loop(lo + 1 + k, hi - 1 - k)
        def _(r):
            raise_row(k, r)

    left(2)
    start(4)
    left(3)
    arrived(1)

    pairs = [(i, j) for i in range(BASIS) for j in range(i, BASIS)]

    def gram_row(r, acc):
        acc = list(acc)
        for b in range(blocks):
            here = pl.ds(b * LANES, LANES)
            x = [[V[k, c, r, :, here] for c in range(2)] for k in range(BASIS)]
            slot = 0
            for i, j in pairs:
                a, z = x[i], x[j]
                acc[slot] = acc[slot] + (a[0] * z[0] + a[1] * z[1])
                slot += 1
                if i != j:
                    acc[slot] = acc[slot] + (a[0] * z[1] - a[1] * z[0])
                    slot += 1
        return tuple(acc)

    count = BASIS * BASIS
    zero = jnp.zeros((waves, LANES), jnp.float32)

    def stage(j, acc):
        arrived(1 + j)

        for k in range(DEPTH):
            d = j - 1 - k

            @pl.loop(0, 2)
            def _(i):
                raise_row(k, lo - d + i * (rows - 1 + 2 * d))

        def near(i, acc):
            d = DEPTH - j
            return gram_row(lo + d + i * (rows - 1 - 2 * d), acc)

        return lax.fori_loop(0, 2, near, acc)

    acc = lax.fori_loop(1, 2, stage, (zero,) * count)
    left(4)
    start(5)
    acc = lax.fori_loop(2, DEPTH + 1, stage, acc)
    packed = zero
    for i in range(count):
        packed = jnp.where(lane == i, jnp.sum(acc[i], axis=1, keepdims=True), packed)
    group = LANES // 32
    spread = zero
    for g in range(group):
        moved = packed if g == 0 else pltpu.roll(packed, 32 * g, 1)
        spread = jnp.where(lax.rem(wave_row, group) == g, moved, spread)
    for q in range(waves // group):
        mine = jnp.logical_and(wave_row >= q * group, wave_row < (q + 1) * group)
        part_out[q : q + 1, :] = jnp.sum(jnp.where(mine, spread, 0.0), axis=0, keepdims=True)
    part_in[me] = part_out[...]

    def sum_copy(d, target):
        return pltpu.make_async_remote_copy(
            src_ref=part_out, dst_ref=part_in.at[me], send_sem=sum_send.at[d],
            recv_sem=sum_recv.at[me], device_id=(part, target), device_id_type=MESH,
        )

    def sum_arrival(source):
        return pltpu.make_async_remote_copy(
            src_ref=part_out, dst_ref=part_in.at[source], send_sem=sum_send.at[0],
            recv_sem=sum_recv.at[source], device_id=(part, source), device_id_type=MESH,
        )

    @pl.loop(1, n)
    def _(d):
        sum_copy(d, lax.rem(me + d, n)).start()

    left(1)
    left(5)

    @pl.loop(1, n)
    def _(d):
        sum_arrival(lax.rem(me + d, n)).wait_recv()

    summed = part_in[0]
    for i in range(1, n):
        summed = summed + part_in[i]
    whole = zero
    for w in range(waves):
        row = jnp.broadcast_to(summed[w // group : w // group + 1, :], (waves, LANES))
        back = (LANES - 32 * (w % group)) % LANES
        whole = jnp.where(wave_row == w, pltpu.roll(row, back, 1) if back else row, whole)
    gram, slot = {}, 0
    for i, j in pairs:
        re = jnp.broadcast_to(whole[:, slot : slot + 1], (waves, LANES))
        slot += 1
        im = zero
        if i != j:
            im = jnp.broadcast_to(whole[:, slot : slot + 1], (waves, LANES))
            slot += 1
        gram[(i, j)] = (re, im)
    weights = krylov_weights(gram, zero + 1.0, zero)
    k2m = -2.0 * k2

    for b in range(blocks):
        here = pl.ds(b * LANES, LANES)
        grad = []
        for r in range(rows):
            x = (S[0, r + 1, :, here], S[1, r + 1, :, here])
            for k, wk in enumerate(weights):
                x = cadd(x, cmul(wk, (V[k, 0, lo + r, :, here], V[k, 1, lo + r, :, here])))
            V[0, 0, lo + r, :, here] = x[0]
            V[0, 1, lo + r, :, here] = x[1]
            g = k2m * (x[0] * F[0, r, :, here] - x[1] * F[1, r, :, here])
            grad.append(jnp.sum(g, axis=0, keepdims=True))
        tile = jnp.concatenate(grad, axis=0)
        for q in range(LANES // width):
            tiles[b * (LANES // width) + q] = tile[:, q * width : (q + 1) * width]

    for o in range(n):
        ordered[o] = tiles[tile_of[o]]

    def tile_copy(d, target):
        return pltpu.make_async_remote_copy(
            src_ref=ordered.at[target], dst_ref=tiles_in.at[me], send_sem=tile_send.at[d],
            recv_sem=tile_recv.at[me], device_id=(part, target), device_id_type=MESH,
        )

    def tile_arrival(source):
        return pltpu.make_async_remote_copy(
            src_ref=ordered.at[source], dst_ref=tiles_in.at[source], send_sem=tile_send.at[0],
            recv_sem=tile_recv.at[source], device_id=(part, source), device_id_type=MESH,
        )

    @pl.loop(1, n)
    def _(d):
        tile_copy(d, lax.rem(me + d, n)).start()

    tiles_in[me] = ordered[me]

    @pl.loop(0, blocks)
    def _(b):
        for c in range(2):
            adj_out[c, :, :, at(b)] = jnp.swapaxes(V[0, c, pl.ds(lo, rows), :, at(b)], 0, 1)

    @pl.loop(1, n)
    def _(d):
        sum_copy(d, lax.rem(me + d, n)).wait_send()

    @pl.loop(1, n)
    def _(d):
        tile_arrival(lax.rem(me + d, n)).wait_recv()

    @pl.loop(1, n)
    def _(d):
        tile_copy(d, lax.rem(me + d, n)).wait_send()

    for r in range(rows):
        grad_out[0, :, r * width : (r + 1) * width] = tiles_in[:, r, :]


def local(
    forward_field, adjoint_start, permittivity, wavenumbers, monitor_cells, pml_widths, owner_map
):
    n = lax.axis_size("space")
    _, waves, rows, cols = adjoint_start.shape
    width = cols // n
    span = rows + 2 * DEPTH
    f32 = jnp.float32
    vmem = pl.BlockSpec(memory_space=pltpu.VMEM)
    smem = pl.BlockSpec(memory_space=pltpu.SMEM)
    hbm = pl.BlockSpec(memory_space=pltpu.HBM)
    dma = pltpu.SemaphoreType.DMA
    return pl.pallas_call(
        functools.partial(kernel, n),
        out_shape=(
            jax.ShapeDtypeStruct(adjoint_start.shape, f32),
            jax.ShapeDtypeStruct((1, n, rows * width), f32),
        ),
        in_specs=[hbm, hbm, hbm, smem, vmem, smem, smem],
        out_specs=(vmem, vmem),
        scratch_shapes=[
            pltpu.VMEM((2, waves, rows, cols), f32),
            pltpu.VMEM((2, waves, rows, cols), f32),
            pltpu.VMEM((rows, cols), f32),
            pltpu.VMEM((2, rows + 2, waves, cols), f32),
            pltpu.VMEM((2, rows, waves, cols), f32),
            pltpu.VMEM((BASIS, 2, span, waves, cols), f32),
            pltpu.VMEM((span, 1, cols), f32),
            pltpu.VMEM((rows, 1, cols), f32),
            pltpu.VMEM((6, span, LANES), f32),
            pltpu.VMEM((2, 6, 8, LANES), f32),
            pltpu.VMEM((waves * 32 // LANES, LANES), f32),
            pltpu.VMEM((n, waves * 32 // LANES, LANES), f32),
            pltpu.VMEM((n, rows, width), f32),
            pltpu.VMEM((n, rows, width), f32),
            pltpu.VMEM((n, rows, width), f32),
            pltpu.SMEM((n,), jnp.int32),
            dma((4,)),
            dma((2 * DEPTH + 4,)),
            dma((2 * DEPTH + 4,)),
            dma((n,)),
            dma((n,)),
            dma((n,)),
            dma((n,)),
        ],
        compiler_params=pltpu.CompilerParams(
            collective_id=0, has_side_effects=True, vmem_limit_bytes=40 * 1024 * 1024
        ),
    )(
        forward_field,
        adjoint_start,
        permittivity,
        wavenumbers.reshape(1, -1),
        monitor_cells.reshape(1, -1),
        pml_widths.reshape(1, -1),
        owner_map,
    )


def solution(mesh):
    placed = (
        P(None, "parts", "space", None),
        P(None, "parts", "space", None),
        P(("parts", "space"), None),
        P("parts"),
        P("parts"),
        P("parts"),
        P(("parts", "space"), None),
    )
    return jax.shard_map(
        local,
        mesh=mesh,
        in_specs=placed,
        out_specs=(P(None, "parts", "space", None), P(("parts", "space"), None, None)),
        check_vma=False,
    )
```

```python
import functools

import jax
import jax.numpy as jnp
from jax import lax
from jax.experimental import pallas as pl
from jax.experimental.pallas import tpu as pltpu
from jax.sharding import PartitionSpec as P

ITERS = 2
SIGMA_PEAK = 4.0
MONITOR_GAIN = 4.0
SHIFT = 4.0
LANES = 128
DEPTH = 4
BASIS = 5
MESH = pl.DeviceIdType.MESH


def stretch(coord, low_width, high_width, total):
    lower_part = jnp.maximum(low_width - coord, 0.0) / low_width
    upper_part = jnp.maximum(coord - (total - 1.0 - high_width), 0.0) / high_width
    damping = SIGMA_PEAK * (
        lower_part * lower_part * lower_part + upper_part * upper_part * upper_part
    )
    denominator = 1.0 + damping * damping
    return (1.0 / denominator, -damping / denominator)


def cmul(a, b):
    return (a[0] * b[0] - a[1] * b[1], a[0] * b[1] + a[1] * b[0])


def cadd(a, b):
    return (a[0] + b[0], a[1] + b[1])


def csub(a, b):
    return (a[0] - b[0], a[1] - b[1])


def cdiv(top, bottom):
    d = bottom[0] * bottom[0] + bottom[1] * bottom[1]
    return (
        (top[0] * bottom[0] + top[1] * bottom[1]) / d,
        (top[1] * bottom[0] - top[0] * bottom[1]) / d,
    )


def three_point(coord, low, high, total):
    below = stretch(coord - 1.0, low, high, total)
    here = stretch(coord, low, high, total)
    above = stretch(coord + 1.0, low, high, total)
    face_low = stretch(coord - 0.5, low, high, total)
    face_high = stretch(coord + 0.5, low, high, total)
    return (
        cmul(face_low, below),
        cmul(cadd(face_low, face_high), here),
        cmul(face_high, above),
    )


def poly_dot(left, right, gram):
    total = None
    for i, a in enumerate(left):
        for j, b in enumerate(right):
            if i <= j:
                g = gram[(i, j)]
            else:
                g = (gram[(j, i)][0], -gram[(j, i)][1])
            term = cmul(cmul((a[0], -a[1]), b), g)
            total = term if total is None else cadd(total, term)
    return total


def poly_energy(q, gram):
    total = None
    for i, a in enumerate(q):
        term = (a[0] * a[0] + a[1] * a[1]) * gram[(i, i)][0]
        total = term if total is None else total + term
        for j in range(i + 1, len(q)):
            b = q[j]
            c_re = a[0] * b[0] + a[1] * b[1]
            c_im = a[0] * b[1] - a[1] * b[0]
            g = gram[(i, j)]
            total = total + 2.0 * (c_re * g[0] - c_im * g[1])
    return total


def poly_scale(c, p):
    return [cmul(c, a) for a in p]


def poly_add(p, q):
    out = []
    for i in range(max(len(p), len(q))):
        if i >= len(p):
            out.append(q[i])
        elif i >= len(q):
            out.append(p[i])
        else:
            out.append(cadd(p[i], q[i]))
    return out


def poly_sub(p, q):
    return poly_add(p, [(-a[0], -a[1]) for a in q])


def poly_image(p):
    raised = [None] + list(p)
    out = []
    for i in range(len(p) + 1):
        if i == 0:
            out.append((SHIFT * p[0][0], SHIFT * p[0][1]))
        elif i == len(p):
            out.append(raised[i])
        else:
            out.append((raised[i][0] + SHIFT * p[i][0], raised[i][1] + SHIFT * p[i][1]))
    return out


def krylov_weights(gram, one, zero):
    unit = (one, zero)
    residual = [unit]
    image = poly_image(residual)
    update = None
    quasi, first_dir, search = residual, residual, image
    direction = None
    start_sq = gram[(0, 0)][0]
    tau = jnp.sqrt(start_sq)
    theta, eta = zero, (zero, zero)
    rho = (start_sq, zero)

    def advance(norm_sq, tau, theta, eta, step, direction, guide, update):
        if direction is None:
            direction = guide
        else:
            ratio = cdiv(eta, step)
            coef = (theta * theta * ratio[0], theta * theta * ratio[1])
            direction = poly_add(guide, poly_scale(coef, direction))
        theta = jnp.sqrt(norm_sq) / tau
        shrink = 1.0 / (1.0 + theta * theta)
        tau = tau * theta * jnp.sqrt(shrink)
        eta = (shrink * step[0], shrink * step[1])
        move = poly_scale(eta, direction)
        update = move if update is None else poly_add(update, move)
        return direction, tau, theta, eta, update

    for iteration in range(ITERS):
        step = cdiv(rho, poly_dot(residual, search, gram))
        quasi = poly_sub(quasi, poly_scale(step, image))
        norm_sq = jnp.maximum(poly_energy(quasi, gram), 0.0)
        direction, tau, theta, eta, update = advance(
            norm_sq, tau, theta, eta, step, direction, first_dir, update
        )
        second_dir = poly_sub(first_dir, poly_scale(step, search))
        second_image = poly_image(second_dir)
        quasi = poly_sub(quasi, poly_scale(step, second_image))
        norm_sq = jnp.maximum(poly_energy(quasi, gram), 0.0)
        direction, tau, theta, eta, update = advance(
            norm_sq, tau, theta, eta, step, direction, second_dir, update
        )
        if iteration + 1 < ITERS:
            rho_new = poly_dot(residual, quasi, gram)
            beta = cdiv(rho_new, rho)
            rho = rho_new
            first_dir = poly_add(quasi, poly_scale(beta, second_dir))
            image = poly_image(first_dir)
            search = poly_add(
                image, poly_scale(beta, poly_add(second_image, poly_scale(beta, search)))
            )
    return update


def kernel(
    n, f_hbm, s_hbm, eps_hbm, wave_in, cell_in, pml_in, owner_in, adj_out, grad_out,
    f_in, s_in, eps_in, S, F, V, E, CN, RC, CC, part_out, part_in, tiles, ordered, tiles_in,
    tile_of, load_sem, edge_send, edge_recv, sum_send, sum_recv, tile_send, tile_recv,
):
    waves, rows, cols = s_in.shape[1], s_in.shape[2], s_in.shape[3]
    blocks = cols // LANES
    width = cols // n
    me = lax.axis_index("space")
    part = lax.axis_index("parts")
    first = me * rows
    total = rows * n
    up, down = me - 1, me + 1
    has_up, has_down = me > 0, me < n - 1

    load_f = [
        pltpu.make_async_copy(f_hbm.at[c], f_in.at[c], load_sem.at[5 * c]) for c in range(2)
    ]
    load_eps = pltpu.make_async_copy(eps_hbm, eps_in, load_sem.at[1])
    half = waves // 2
    load_s = [
        [
            pltpu.make_async_copy(
                s_hbm.at[c, pl.ds(h * half, half)],
                s_in.at[c, pl.ds(h * half, half)],
                load_sem.at[6 + 2 * c + h],
            )
            for h in range(2)
        ]
        for c in range(2)
    ]
    for pair in load_s:
        for load in pair:
            load.start()

    barrier = pltpu.get_barrier_semaphore()

    @pl.loop(1, n)
    def _(d):
        pl.semaphore_signal(
            barrier, inc=1, device_id=(part, lax.rem(me + d, n)), device_id_type=MESH
        )

    def at(b):
        return pl.ds(pl.multiple_of(b * LANES, LANES), LANES)

    for c in range(2):
        load_s[c][0].wait()
        load_s[c][1].wait()

        @pl.loop(0, blocks)
        def _(b):
            S[c, pl.ds(1, rows), :, at(b)] = jnp.swapaxes(s_in[c, :, :, at(b)], 0, 1)

    def edge(slot, src, dst, target):
        return pltpu.make_async_remote_copy(
            src_ref=src, dst_ref=dst, send_sem=edge_send.at[slot], recv_sem=edge_recv.at[slot],
            device_id=(part, target), device_id_type=MESH,
        )

    V0 = V.at[0]
    lo, hi = DEPTH, DEPTH + rows
    reach = DEPTH - 1
    slots = DEPTH + 2

    def to_up(i):
        if isinstance(i, int) and i == 0:
            return edge(0, S.at[:, 1], S.at[:, rows + 1], up)
        if isinstance(i, int) and i == 1:
            return edge(1, E.at[pl.ds(lo, reach)], E.at[pl.ds(hi, reach)], up)
        return edge(i, V0.at[:, lo + i - 2], V0.at[:, hi + i - 2], up)

    def to_down(i):
        if isinstance(i, int) and i == 0:
            return edge(slots, S.at[:, rows], S.at[:, 0], down)
        if isinstance(i, int) and i == 1:
            return edge(
                slots + 1, E.at[pl.ds(hi - reach, reach)], E.at[pl.ds(lo - reach, reach)], down
            )
        return edge(slots + i, V0.at[:, hi + 1 - i], V0.at[:, lo + 1 - i], down)

    def start(i):
        @pl.when(has_up)
        def _():
            to_up(i).start()

        @pl.when(has_down)
        def _():
            to_down(i).start()

    def arrived(i):
        @pl.when(has_up)
        def _():
            to_down(i).wait_recv()

        @pl.when(has_down)
        def _():
            to_up(i).wait_recv()

    def left(i):
        @pl.when(has_up)
        def _():
            to_up(i).wait_send()

        @pl.when(has_down)
        def _():
            to_down(i).wait_send()

    load_eps.start()
    load_f[0].start()
    load_f[1].start()
    pl.semaphore_wait(barrier, n - 1)
    start(0)

    @pl.when(jnp.logical_not(has_up))
    def _():
        S[:, 0] = jnp.zeros((2, waves, cols), jnp.float32)
        E[pl.ds(0, DEPTH)] = jnp.zeros((DEPTH, 1, cols), jnp.float32)
        V[0, :, pl.ds(0, DEPTH)] = jnp.zeros((2, DEPTH, waves, cols), jnp.float32)

    @pl.when(jnp.logical_not(has_down))
    def _():
        S[:, rows + 1] = jnp.zeros((2, waves, cols), jnp.float32)
        E[pl.ds(hi, DEPTH)] = jnp.zeros((DEPTH, 1, cols), jnp.float32)
        V[0, :, pl.ds(hi, DEPTH)] = jnp.zeros((2, DEPTH, waves, cols), jnp.float32)

    load_eps.wait()
    for r in range(rows):
        E[DEPTH + r] = eps_in[pl.ds(r, 1), :]
    start(1)

    load_f[0].wait()
    load_f[1].wait()

    @pl.loop(0, blocks)
    def _(b):
        for c in range(2):
            F[c, :, :, at(b)] = jnp.swapaxes(f_in[c, :, :, at(b)], 0, 1)

    wid = [pml_in[0, i].astype(jnp.float32) for i in range(4)]
    span = rows + 2 * DEPTH
    row_id = lax.broadcasted_iota(jnp.int32, (span, LANES), 0) + (first - DEPTH)
    inside = jnp.logical_and(row_id >= 0, row_id <= total - 1)
    am, a0, ap = three_point(row_id.astype(jnp.float32), wid[0], wid[1], total)
    for i, x in enumerate((am, a0, ap)):
        for c in range(2):
            RC[2 * i + c] = jnp.where(inside, x[c], 0.0)
    RC[2] = jnp.where(inside, a0[0], 0.0) + (2.0 - SHIFT)
    for e, base in enumerate((0, cols - LANES)):
        col_id = (lax.broadcasted_iota(jnp.int32, (8, LANES), 1) + base).astype(jnp.float32)
        bm, b0, bp = three_point(col_id, wid[2], wid[3], cols)
        for i, x in enumerate((bm, b0, bp)):
            for c in range(2):
                CC[e, 2 * i + c] = x[c]
        CC[e, 2] = b0[0] - 2.0

    wave_row = lax.broadcasted_iota(jnp.int32, (waves, LANES), 0)
    k2 = jnp.zeros((waves, LANES), jnp.float32)
    for w in range(waves):
        k2 = jnp.where(wave_row == w, wave_in[0, w], k2)
    k2 = k2 * k2

    m = cell_in.shape[1]
    cells = cell_in[...]
    bits = cols.bit_length() - 1
    cell_rows = lax.shift_right_logical(cells, bits)
    cell_cols = jnp.bitwise_and(cells, cols - 1).astype(jnp.float32)
    rows_hot = (
        cell_rows == lax.broadcasted_iota(jnp.int32, (rows, m), 0) + first
    ).astype(jnp.float32)
    diag = lax.broadcasted_iota(jnp.int32, (m, m), 0) == lax.broadcasted_iota(jnp.int32, (m, m), 1)
    col_at = jnp.sum(
        jnp.where(diag, jnp.broadcast_to(cell_cols, (m, m)), 0.0), axis=1, keepdims=True
    ).astype(jnp.int32)
    cols_hot = (col_at == lax.broadcasted_iota(jnp.int32, (m, cols), 1)).astype(jnp.float32)
    counts = jnp.dot(rows_hot, cols_hot, preferred_element_type=jnp.float32)
    for r in range(rows):
        CN[r] = MONITOR_GAIN * counts[r : r + 1]

    lane = lax.broadcasted_iota(jnp.int32, (waves, LANES), 1)
    is_first, is_last = lane == 0, lane == LANES - 1

    def shifted_image(src, t, r, emit):
        co = [
            jnp.broadcast_to(RC[i, pl.ds(r, 1), :], (waves, LANES)) for i in range(6)
        ]
        rolled = {}

        def get(b):
            if b not in rolled:
                x = [src[c, t, :, pl.ds(b * LANES, LANES)] for c in range(2)]
                rolled[b] = (
                    x,
                    [pltpu.roll(y, 1, 1) for y in x],
                    [pltpu.roll(y, LANES - 1, 1) for y in x],
                )
            return rolled[b]

        for b in range(blocks):
            here = pl.ds(b * LANES, LANES)
            v, r_left, r_right = get(b)
            before = get(b - 1)[1] if b > 0 else (0.0, 0.0)
            after = get(b + 1)[2] if b + 1 < blocks else (0.0, 0.0)
            lf = [jnp.where(is_first, before[c], r_left[c]) for c in range(2)]
            rt = [jnp.where(is_last, after[c], r_right[c]) for c in range(2)]
            above = [src[c, t - 1, :, here] for c in range(2)]
            below = [src[c, t + 1, :, here] for c in range(2)]
            mass = k2 * E[r, :, here]
            d = (co[2] - mass, co[3])
            if b == 0 or b == blocks - 1:
                e = 0 if b == 0 else 1
                cc = [CC[e, i] for i in range(6)]
                d = (d[0] + cc[2], d[1] + cc[3])
                side = cadd(cmul((cc[0], cc[1]), lf), cmul((cc[4], cc[5]), rt))
            else:
                side = cadd(lf, rt)
            out = csub(
                csub(cmul(d, v), side),
                cadd(cmul((co[0], co[1]), above), cmul((co[4], co[5]), below)),
            )
            emit(b, here, v, out)
            rolled.pop(b - 1, None)

    def residual_row(r):
        def emit(b, here, v, out):
            gain = CN[r, :, here]
            V[0, 0, DEPTH + r, :, here] = -gain * F[0, r, :, here] - (out[0] + SHIFT * v[0])
            V[0, 1, DEPTH + r, :, here] = gain * F[1, r, :, here] - (out[1] + SHIFT * v[1])

        shifted_image(S, r + 1, DEPTH + r, emit)

    def raise_row(k, r):
        def emit(b, here, v, out):
            V[k + 1, 0, r, :, here] = out[0]
            V[k + 1, 1, r, :, here] = out[1]

        shifted_image(V.at[k], r, r, emit)

    @pl.loop(0, 2)
    def _(i):
        residual_row(1 + i * (rows - 3))

    @pl.loop(2, rows - 2)
    def _(r):
        residual_row(r)

    left(0)
    arrived(0)

    @pl.loop(0, 2)
    def _(i):
        residual_row(i * (rows - 1))

    start(2)
    start(3)

    @pl.loop(0, n)
    def _(o):
        def count(k, found):
            return jnp.where(owner_in[0, k] == o, k, found)

        tile_of[o] = lax.fori_loop(0, n, count, jnp.int32(0), unroll=True)

    for k in range(DEPTH - 1):
        @pl.loop(lo + 1 + k, hi - 1 - k)
        def _(r):
            raise_row(k, r)

    left(2)
    start(4)
    left(3)
    arrived(1)

    pairs = [(i, j) for i in range(BASIS) for j in range(i, BASIS)]

    def gram_row(r, acc):
        acc = list(acc)
        for b in range(blocks):
            here = pl.ds(b * LANES, LANES)
            x = [[V[k, c, r, :, here] for c in range(2)] for k in range(BASIS)]
            slot = 0
            for i, j in pairs:
                a, z = x[i], x[j]
                acc[slot] = acc[slot] + (a[0] * z[0] + a[1] * z[1])
                slot += 1
                if i != j:
                    acc[slot] = acc[slot] + (a[0] * z[1] - a[1] * z[0])
                    slot += 1
        return tuple(acc)

    count = BASIS * BASIS
    zero = jnp.zeros((waves, LANES), jnp.float32)

    def stage(j, acc):
        arrived(1 + j)

        for k in range(DEPTH):
            d = j - 1 - k

            @pl.loop(0, 2)
            def _(i):
                raise_row(k, lo - d + i * (rows - 1 + 2 * d))

        def near(i, acc):
            d = DEPTH - j
            return gram_row(lo + d + i * (rows - 1 - 2 * d), acc)

        return lax.fori_loop(0, 2, near, acc)

    acc = lax.fori_loop(1, 2, stage, (zero,) * count)
    left(4)
    start(5)
    acc = lax.fori_loop(2, DEPTH + 1, stage, acc)
    packed = zero
    for i in range(count):
        packed = jnp.where(lane == i, jnp.sum(acc[i], axis=1, keepdims=True), packed)
    group = LANES // 32
    spread = zero
    for g in range(group):
        moved = packed if g == 0 else pltpu.roll(packed, 32 * g, 1)
        spread = jnp.where(lax.rem(wave_row, group) == g, moved, spread)
    for q in range(waves // group):
        mine = jnp.logical_and(wave_row >= q * group, wave_row < (q + 1) * group)
        part_out[q : q + 1, :] = jnp.sum(jnp.where(mine, spread, 0.0), axis=0, keepdims=True)
    part_in[me] = part_out[...]

    def sum_copy(d, target):
        return pltpu.make_async_remote_copy(
            src_ref=part_out, dst_ref=part_in.at[me], send_sem=sum_send.at[d],
            recv_sem=sum_recv.at[me], device_id=(part, target), device_id_type=MESH,
        )

    def sum_arrival(source):
        return pltpu.make_async_remote_copy(
            src_ref=part_out, dst_ref=part_in.at[source], send_sem=sum_send.at[0],
            recv_sem=sum_recv.at[source], device_id=(part, source), device_id_type=MESH,
        )

    @pl.loop(1, n)
    def _(d):
        sum_copy(d, lax.rem(me + d, n)).start()

    left(1)
    left(5)

    @pl.loop(1, n)
    def _(d):
        sum_arrival(lax.rem(me + d, n)).wait_recv()

    summed = part_in[0]
    for i in range(1, n):
        summed = summed + part_in[i]
    whole = zero
    for w in range(waves):
        row = jnp.broadcast_to(summed[w // group : w // group + 1, :], (waves, LANES))
        back = (LANES - 32 * (w % group)) % LANES
        whole = jnp.where(wave_row == w, pltpu.roll(row, back, 1) if back else row, whole)
    gram, slot = {}, 0
    for i, j in pairs:
        re = jnp.broadcast_to(whole[:, slot : slot + 1], (waves, LANES))
        slot += 1
        im = zero
        if i != j:
            im = jnp.broadcast_to(whole[:, slot : slot + 1], (waves, LANES))
            slot += 1
        gram[(i, j)] = (re, im)
    weights = krylov_weights(gram, zero + 1.0, zero)
    k2m = -2.0 * k2

    for b in range(blocks):
        here = pl.ds(b * LANES, LANES)
        grad = []
        for r in range(rows):
            x = (S[0, r + 1, :, here], S[1, r + 1, :, here])
            for k, wk in enumerate(weights):
                x = cadd(x, cmul(wk, (V[k, 0, lo + r, :, here], V[k, 1, lo + r, :, here])))
            V[0, 0, lo + r, :, here] = x[0]
            V[0, 1, lo + r, :, here] = x[1]
            g = k2m * (x[0] * F[0, r, :, here] - x[1] * F[1, r, :, here])
            grad.append(jnp.sum(g, axis=0, keepdims=True))
        tile = jnp.concatenate(grad, axis=0)
        for q in range(LANES // width):
            tiles[b * (LANES // width) + q] = tile[:, q * width : (q + 1) * width]

    for o in range(n):
        ordered[o] = tiles[tile_of[o]]

    def tile_copy(d, target):
        return pltpu.make_async_remote_copy(
            src_ref=ordered.at[target], dst_ref=tiles_in.at[me], send_sem=tile_send.at[d],
            recv_sem=tile_recv.at[me], device_id=(part, target), device_id_type=MESH,
        )

    def tile_arrival(source):
        return pltpu.make_async_remote_copy(
            src_ref=ordered.at[source], dst_ref=tiles_in.at[source], send_sem=tile_send.at[0],
            recv_sem=tile_recv.at[source], device_id=(part, source), device_id_type=MESH,
        )

    @pl.loop(1, n)
    def _(d):
        tile_copy(d, lax.rem(me + d, n)).start()

    tiles_in[me] = ordered[me]

    @pl.loop(0, blocks)
    def _(b):
        for c in range(2):
            adj_out[c, :, :, at(b)] = jnp.swapaxes(V[0, c, pl.ds(lo, rows), :, at(b)], 0, 1)

    @pl.loop(1, n)
    def _(d):
        sum_copy(d, lax.rem(me + d, n)).wait_send()

    @pl.loop(1, n)
    def _(d):
        tile_arrival(lax.rem(me + d, n)).wait_recv()

    @pl.loop(1, n)
    def _(d):
        tile_copy(d, lax.rem(me + d, n)).wait_send()

    for r in range(rows):
        grad_out[0, :, r * width : (r + 1) * width] = tiles_in[:, r, :]


def local(
    forward_field, adjoint_start, permittivity, wavenumbers, monitor_cells, pml_widths, owner_map
):
    n = lax.axis_size("space")
    _, waves, rows, cols = adjoint_start.shape
    width = cols // n
    span = rows + 2 * DEPTH
    f32 = jnp.float32
    vmem = pl.BlockSpec(memory_space=pltpu.VMEM)
    smem = pl.BlockSpec(memory_space=pltpu.SMEM)
    hbm = pl.BlockSpec(memory_space=pltpu.HBM)
    dma = pltpu.SemaphoreType.DMA
    return pl.pallas_call(
        functools.partial(kernel, n),
        out_shape=(
            jax.ShapeDtypeStruct(adjoint_start.shape, f32),
            jax.ShapeDtypeStruct((1, n, rows * width), f32),
        ),
        in_specs=[hbm, hbm, hbm, smem, vmem, smem, smem],
        out_specs=(vmem, vmem),
        scratch_shapes=[
            pltpu.VMEM((2, waves, rows, cols), f32),
            pltpu.VMEM((2, waves, rows, cols), f32),
            pltpu.VMEM((rows, cols), f32),
            pltpu.VMEM((2, rows + 2, waves, cols), f32),
            pltpu.VMEM((2, rows, waves, cols), f32),
            pltpu.VMEM((BASIS, 2, span, waves, cols), f32),
            pltpu.VMEM((span, 1, cols), f32),
            pltpu.VMEM((rows, 1, cols), f32),
            pltpu.VMEM((6, span, LANES), f32),
            pltpu.VMEM((2, 6, 8, LANES), f32),
            pltpu.VMEM((waves * 32 // LANES, LANES), f32),
            pltpu.VMEM((n, waves * 32 // LANES, LANES), f32),
            pltpu.VMEM((n, rows, width), f32),
            pltpu.VMEM((n, rows, width), f32),
            pltpu.VMEM((n, rows, width), f32),
            pltpu.SMEM((n,), jnp.int32),
            dma((10,)),
            dma((2 * DEPTH + 4,)),
            dma((2 * DEPTH + 4,)),
            dma((n,)),
            dma((n,)),
            dma((n,)),
            dma((n,)),
        ],
        compiler_params=pltpu.CompilerParams(
            collective_id=0, has_side_effects=True, vmem_limit_bytes=40 * 1024 * 1024
        ),
    )(
        forward_field,
        adjoint_start,
        permittivity,
        wavenumbers.reshape(1, -1),
        monitor_cells.reshape(1, -1),
        pml_widths.reshape(1, -1),
        owner_map,
    )


def solution(mesh):
    placed = (
        P(None, "parts", "space", None),
        P(None, "parts", "space", None),
        P(("parts", "space"), None),
        P("parts"),
        P("parts"),
        P("parts"),
        P(("parts", "space"), None),
    )
    return jax.shard_map(
        local,
        mesh=mesh,
        in_specs=placed,
        out_specs=(P(None, "parts", "space", None), P(("parts", "space"), None, None)),
        check_vma=False,
    )
```
